32 devices in a mesh: groups: 2 (over x), wide: 16 (over z, y, core).
Axes of the slice: x: 2, y: 2, z: 4, core: 2. Of those that a mesh axis runs over, the one named last changes fastest.
Arguments:
- iterate: float32 [8192, 128], P(('groups', 'wide')), parts along dimension 0, may hold values from -6 to 6
- rhs: float32 [8192, 128], P(('groups', 'wide')), parts along dimension 0, may hold values from -6 to 6
- schur: float32 [32, 384, 384], P(('groups', 'wide')), parts along dimension 0
- near_block: float32 [8192, 256], P(('groups', 'wide')), parts along dimension 0
- u_basis: float32 [32, 32, 4096], P('groups', None, 'wide'), parts along dimension 0, may hold values from -0.375 to 0.375
- v_basis: float32 [32, 32, 4096], P('groups', None, 'wide'), parts along dimension 0, may hold values from -0.375 to 0.375
- tile_rank: int32 [32, 16], P('groups', 'wide'), parts along dimension 0, may hold values from 1 to 32
- send_rows: int32 [32, 3, 128], P(('groups', 'wide')), parts along dimension 0, may hold values from 0 to 255
- send_count: int32 [32, 3], P(('groups', 'wide')), parts along dimension 0, may hold values from 0 to 128, as said below
- precond: float32 [8192], P(('groups', 'wide')), parts along dimension 0, may hold values from 0.1 to 1
Outputs:
- updated: float32 [8192, 128], P(('groups', 'wide')), parts along dimension 0
- residual: float32 [8192, 128], P(('groups', 'wide')), parts along dimension 0
The draws below stay inside these ranges and needn't reach their ends.
There are 2 independent parts, one for each index of `groups`. The reference program is written for one: setup_inputs(seed, part) draws one part's arguments, and reference() takes and returns one part's arrays. A program takes and returns all parts, laid end to end along the dimension named above; each array names one. Nothing has to cross between parts.
Inputs may be any that keep to these rules, and one draw needn't show every extreme that they name: send_count[p, 0] is 0 for p = 0 and send_count[p, 2] is 0 for p = 15; a block is full in every draw.
All inputs are finite; a program needn't handle non-finite values.
Results may differ from the reference program's by a relative error of at most 0.0003.
Values sent between devices are 32-bit elements; how exact they have to be, the bound alone decides.
No kernel may reach another device: no remote copies, remote signals or barrier semaphores. Data moves between devices by JAX's collectives and lax.ppermute only.
A program may use at most 64 MiB of HBM per device.

```python
import math
import jax
import jax.numpy as jnp
from jax import lax

R_DEV = 256
LOADS = 128
K = 32
FB = 128
NS = 384
TILES = 16
N = 4096


def draw_schur(key, part):
    key_off = jax.random.fold_in(key, 11)
    key_diag = jax.random.fold_in(key, 12)
    off_diag = jax.random.normal(key_off, (TILES, NS, NS), jnp.float32)
    off_diag = off_diag * (0.5 / jnp.sqrt(jnp.float32(NS)))
    diag = jax.random.uniform(key_diag, (TILES, NS), jnp.float32, 1.5, 3.0)
    return off_diag + diag[:, :, None] * jnp.eye(NS, dtype=jnp.float32)[None]


def draw_near_block(key, part):
    key_off = jax.random.fold_in(key, 21)
    key_diag = jax.random.fold_in(key, 22)
    off_diag = jax.random.normal(key_off, (N, R_DEV), jnp.float32)
    off_diag = off_diag * (0.5 / jnp.sqrt(jnp.float32(R_DEV)))
    diag = jax.random.uniform(key_diag, (N, 1), jnp.float32, 0.5, 1.5)
    eye_rows = jnp.tile(jnp.eye(R_DEV, dtype=jnp.float32), (TILES, 1))
    return off_diag + diag * eye_rows


def draw_tile_rank(key, part):
    ranks = jax.random.randint(jax.random.fold_in(key, 31), (TILES, TILES), 1, K + 1, dtype=jnp.int32)
    return ranks.at[0, 1].set(1).at[1, 0].set(K)


def draw_send_count(key, part):
    counts = jax.random.randint(jax.random.fold_in(key, 41), (TILES, 3), 0, FB + 1, dtype=jnp.int32)
    owner = jnp.arange(TILES, dtype=jnp.int32)[:, None]
    offset = jnp.arange(3, dtype=jnp.int32)[None, :] - 1
    target = owner + offset
    inside = (target >= 0) & (target < TILES)
    counts = jnp.where(inside, counts, 0)
    return counts.at[1, 1].set(FB)


def touch_ends(drawn, stream_key, low, high):
    longest = drawn.shape.index(max(drawn.shape))
    spots = []
    for shift in (0, 1):
        where = [jax.random.randint(jax.random.fold_in(stream_key, axis), (), 0, length) for axis, length in enumerate(drawn.shape)]
        where[longest] = (where[longest] + shift) % drawn.shape[longest]
        spots.append(tuple(where))
    return drawn.at[spots[0]].set(low).at[spots[1]].set(high)


def raised(drawn, key, source, target, parts, factor):
    def block_of(axis_at):
        return (jnp.arange(drawn.shape[axis_at]) // (drawn.shape[axis_at] // parts)).reshape((-1,) + (1,) * (drawn.ndim - 1 - axis_at))

    one_side = jax.random.permutation(key, parts)[block_of(target)]
    second = (block_of(target) + parts // 2) % parts
    return jnp.where((block_of(source) == one_side) | (block_of(source) == second), factor * drawn, drawn)


def block_scale(rng, shape, shards, smallest, high):
    factor_of = 1.0
    for dim, blocks in shards:
        heights = jax.random.uniform(jax.random.fold_in(jax.random.fold_in(rng, 6), dim), (blocks,), jnp.float32, smallest / len(shards), high / len(shards))
        factor_of = factor_of * jnp.repeat(jnp.exp(heights), shape[dim] // blocks).reshape((-1,) + (1,) * (len(shape) - 1 - dim))
    return factor_of


def scatter_about(rng, shape, width, limit, split=(), kind=jnp.bfloat16):
    result = jax.random.normal(rng, shape, jnp.float32) * width
    if len(split) > 0:
        result = block_scale(rng, shape, split, -0.22, 0.18) * result
    return jnp.clip(result, min=-limit, max=limit).astype(kind)


def noise_with(stream_key, extent, spread, bound, split, heavy, held_as=jnp.bfloat16):
    entries = spread * jax.random.normal(stream_key, extent, jnp.float32)
    if split:
        entries = entries * block_scale(stream_key, extent, split, -0.22, 0.18)
    return jnp.clip(raised(entries, jax.random.fold_in(stream_key, 3), *heavy), -bound, bound).astype(held_as)


def setup_inputs(seed: int = 0, part: int = 0) -> dict:
    splits = jax.random.split(jax.random.key(seed), 11)
    part_splits = jax.random.split(jax.random.fold_in(splits[10], part), 11)
    iterate = scatter_about(part_splits[0], (N, LOADS), 1.0, 6.0, ((0, 16),), jnp.float32)
    rhs = scatter_about(part_splits[1], (N, LOADS), 1.0, 6.0, ((0, 16),), jnp.float32)
    schur = draw_schur(jax.random.fold_in(jax.random.fold_in(splits[10], part), 71), part)
    near_block = draw_near_block(jax.random.fold_in(jax.random.fold_in(splits[10], part), 71), part)
    u_basis = noise_with(part_splits[4], (TILES, K, N), (TILES * K) ** -0.5, 0.375, ((2, 16),), (0, 2, 16, 2.0), jnp.float32)
    v_basis = scatter_about(part_splits[5], (TILES, K, N), R_DEV ** -0.5, 0.375, ((2, 16),), jnp.float32)
    tile_rank = draw_tile_rank(jax.random.fold_in(jax.random.fold_in(splits[10], part), 71), part)
    send_rows = touch_ends(jax.random.randint(part_splits[7], (TILES, 3, FB), 0, R_DEV), jax.random.fold_in(part_splits[7], 1), 0, R_DEV - 1).astype(jnp.int32)
    send_count = draw_send_count(jax.random.fold_in(jax.random.fold_in(splits[10], part), 71), part)
    precond = jnp.clip(jnp.exp(math.log(1.0) - 2.3025851 * jax.random.uniform(part_splits[9], (N,), jnp.float32) ** block_scale(part_splits[9], (N,), ((0, 16),), -0.2, 0.2)), 0.1, 1.0)
    return {"iterate": iterate, "rhs": rhs, "schur": schur, "near_block": near_block, "u_basis": u_basis, "v_basis": v_basis, "tile_rank": tile_rank, "send_rows": send_rows, "send_count": send_count, "precond": precond}


def reference(iterate, rhs, schur, near_block, u_basis, v_basis, tile_rank, send_rows, send_count, precond):
    highest = lax.Precision.HIGHEST
    rows_local = jnp.arange(R_DEV, dtype=jnp.int32)
    slot_ids = jnp.arange(FB, dtype=jnp.int32)
    blocks = iterate.reshape(TILES, R_DEV, LOADS)
    valid = slot_ids[None, None, :] < send_count[:, :, None]
    select = ((send_rows[..., None] == rows_local) & valid[..., None]).astype(iterate.dtype)
    outgoing = jnp.einsum('posr,prl->posl', select, blocks, precision=highest)
    zero_block = jnp.zeros((1, 3, FB, LOADS), iterate.dtype)
    out_pad = jnp.concatenate([zero_block, outgoing, zero_block], axis=0)
    incoming = jnp.stack([out_pad[2:, 0], out_pad[1:-1, 1], out_pad[:-2, 2]], axis=1)
    forces = jnp.einsum('dab,dbl->dal', schur, incoming.reshape(TILES, NS, LOADS), precision=highest)
    forces = forces.reshape(TILES, 3, FB, LOADS)
    force_pad = jnp.concatenate([zero_block, forces, zero_block], axis=0)
    returned = jnp.stack([force_pad[:-2, 0], force_pad[1:-1, 1], force_pad[2:, 2]], axis=1)
    fem = jnp.einsum('posr,posl->prl', select, returned, precision=highest).reshape(N, LOADS)
    rank_ids = jnp.arange(K, dtype=jnp.int32)

    def tile_row(index):
        v_row = v_basis[index].reshape(K, TILES, R_DEV)
        coeff = jnp.einsum('kjr,jrl->jkl', v_row, blocks, precision=highest)
        keep = (rank_ids[None, :] < tile_rank[index][:, None]).astype(iterate.dtype)
        coeff = coeff * keep[:, :, None]
        u_row = lax.dynamic_slice_in_dim(u_basis, index * R_DEV, R_DEV, 2)
        return jnp.einsum('jkr,jkl->rl', u_row, coeff, precision=highest)

    far = lax.map(tile_row, jnp.arange(TILES, dtype=jnp.int32)).reshape(N, LOADS)
    near = jnp.einsum('prs,psl->prl', near_block.reshape(TILES, R_DEV, R_DEV), blocks, precision=highest).reshape(N, LOADS)
    residual = rhs - (fem + (far + near))
    updated = iterate + precond[:, None] * residual
    return updated, residual
```

```python
import functools

import jax
import jax.numpy as jnp
from jax import lax
from jax.experimental import pallas as pl
from jax.experimental.pallas import tpu as pltpu
from jax.sharding import PartitionSpec as P

VMEM = pl.BlockSpec(memory_space=pltpu.VMEM)
SMEM = pl.BlockSpec(memory_space=pltpu.SMEM)
f32 = jnp.float32
bf16 = jnp.bfloat16


def halves(a):
    hi = a.astype(bf16)
    return hi, (a - hi.astype(f32)).astype(bf16)


def dot(a, b):
    return jnp.dot(a, b, preferred_element_type=f32)


def wide_halves(a):
    return jnp.concatenate(halves(a), axis=1)


def product(a, b_wide):
    n = b_wide.shape[1] // 2
    hi, lo = halves(a)
    both = dot(hi, b_wide)
    return both[:, :n] + (both[:, n:] + dot(lo, b_wide[:, :n]))


def face_slot(spot, odd):
    return 1 if spot == 1 else jnp.where(odd == spot // 2, 2, 0)


def live_rows(rows_ref, count_ref, slot):
    rows = rows_ref[pl.ds(slot, 1), :]
    lane = lax.broadcasted_iota(jnp.int32, rows.shape, 1)
    return jnp.where(lane < count_ref[slot], rows, -1)


def send_kernel(rank_ref, count_ref, odd_ref, x_ref, v_ref, rows_ref, coeff_ref, a_ref, m_ref, b_ref):
    loads = x_ref.shape[1]
    n_rows = x_ref.shape[0]
    x_wide = wide_halves(x_ref[...])
    odd = odd_ref[0]
    for spot, out_ref in enumerate((a_ref, m_ref, b_ref)):
        rows = live_rows(rows_ref, count_ref, face_slot(spot, odd))
        local = lax.broadcasted_iota(jnp.int32, (n_rows, rows.shape[1]), 0)
        select = (local == rows).astype(f32).T.astype(bf16)
        both = dot(select, x_wide)
        out_ref[...] = both[:, :loads] + both[:, loads:]
    tiles, top, _ = v_ref.shape
    step = max(1, min(tiles, 256 // top))

    @pl.loop(0, tiles // step, unroll=tiles <= 32)
    def _(s):
        first = s * step
        part = v_ref[pl.ds(first, step)].reshape(step * top, n_rows)
        out = product(part, x_wide).reshape(step, top, loads)
        k = lax.broadcasted_iota(jnp.int32, (top, loads), 0)
        for t in range(step):
            coeff_ref[first + t] = jnp.where(k < rank_ref[first + t], out[t], 0.0)


def schur_kernel(odd_ref, a_ref, m_ref, b_ref, schur_ref, fa_ref, fm_ref, fb_ref):
    odd = odd_ref[0]
    face = a_ref.shape[0]
    is_odd = odd == 1
    a, b = a_ref[...], b_ref[...]
    first = jnp.where(is_odd, b, a)
    last = jnp.where(is_odd, a, b)
    incoming = wide_halves(jnp.concatenate([first, m_ref[...], last], axis=0))
    starts = (jnp.where(is_odd, 2 * face, 0), face, jnp.where(is_odd, 0, 2 * face))
    for start, out_ref in zip(starts, (fa_ref, fm_ref, fb_ref)):
        start = pl.multiple_of(start, face)
        out_ref[...] = product(schur_ref[pl.ds(start, face), :], incoming)


def base_kernel(count_ref, odd_ref, rhs_ref, near_ref, x_ref, rows_ref, fa_ref, fm_ref, fb_ref, u_ref, base_ref, hi_ref, lo_ref):
    n_rows, loads = x_ref.shape
    odd = odd_ref[0]
    total = rhs_ref[...] - product(near_ref[...], wide_halves(x_ref[...]))
    for spot, f_ref in enumerate((fa_ref, fm_ref, fb_ref)):
        rows = live_rows(rows_ref, count_ref, face_slot(spot, odd))
        local = lax.broadcasted_iota(jnp.int32, (n_rows, rows.shape[1]), 0)
        both = dot((local == rows).astype(f32).astype(bf16), wide_halves(f_ref[...]))
        total = total - (both[:, :loads] + both[:, loads:])
    base_ref[...] = total
    ut = u_ref[...].T
    hi_ref[...], lo_ref[...] = halves(ut)


def final_kernel(coeff_ref, hi_ref, lo_ref, base_ref, x_ref, p_ref, up_ref, res_ref):
    loads = x_ref.shape[1]
    c_wide = wide_halves(coeff_ref[...])
    both = dot(hi_ref[...], c_wide)
    far = both[:, :loads] + (both[:, loads:] + dot(lo_ref[...], c_wide[:, :loads]))
    res = base_ref[...] - far
    res_ref[...] = res
    scale = jnp.broadcast_to(p_ref[...], (8, p_ref.shape[1])).T[:, :1]
    up_ref[...] = x_ref[...] + scale * res


def call(kernel, outs, specs, name):
    return pl.pallas_call(
        kernel,
        out_shape=tuple(jax.ShapeDtypeStruct(s, t) for s, t in outs),
        in_specs=specs,
        out_specs=tuple(VMEM for _ in outs),
        compiler_params=pltpu.CompilerParams(vmem_limit_bytes=40 * 2**20),
        name=name,
    )


def body(iterate, rhs, schur, near_block, u_basis, v_basis, tile_rank, send_rows, send_count, precond):
    n_rows, loads = iterate.shape
    face = send_rows.shape[2]
    tiles, top, _ = u_basis.shape
    size = lax.axis_size("wide")
    odd = jnp.reshape(lax.axis_index("wide") % 2, (1,)).astype(jnp.int32)
    inside = [(i, i ^ 1) for i in range(size) if i ^ 1 < size]
    across = [(i, j) for i in range(size) for j in [i - 1 if i % 2 == 0 else i + 1] if 0 <= j < size]
    rank = tile_rank.reshape(tiles)
    count = send_count.reshape(3)
    rows = send_rows.reshape(3, face)
    block = ((face, loads), f32)

    coeff, out_a, out_m, out_b = call(
        send_kernel, [((tiles, top, loads), f32), block, block, block], [SMEM] * 3 + [VMEM] * 3, "send"
    )(rank, count, odd, iterate, v_basis, rows)
    gathered = lax.all_to_all(coeff, "wide", split_axis=0, concat_axis=0, tiled=True)
    in_a = lax.ppermute(out_a, "wide", inside)
    in_b = lax.ppermute(out_b, "wide", across)
    f_a, f_m, f_b = call(schur_kernel, [block] * 3, [SMEM] + [VMEM] * 4, "schur")(
        odd, in_a, out_m, in_b, schur.reshape(3 * face, 3 * face)
    )
    back_a = lax.ppermute(f_a, "wide", inside)
    back_b = lax.ppermute(f_b, "wide", across)
    base, u_hi, u_lo = call(
        base_kernel,
        [((n_rows, loads), f32), ((n_rows, tiles * top), bf16), ((n_rows, tiles * top), bf16)],
        [SMEM] * 2 + [VMEM] * 8,
        "base",
    )(count, odd, rhs, near_block, iterate, rows, back_a, f_m, back_b, u_basis.reshape(tiles * top, n_rows))
    return call(final_kernel, [((n_rows, loads), f32)] * 2, [VMEM] * 6, "final")(
        gathered.reshape(tiles * top, loads), u_hi, u_lo, base, iterate, precond.reshape(1, n_rows)
    )


def solution(mesh):
    rows = P(("groups", "wide"), None)
    block = P(("groups", "wide"), None, None)
    basis = P("groups", None, "wide")
    in_specs = (rows, rows, block, rows, basis, basis, P("groups", "wide"), block, rows, P(("groups", "wide")))
    return jax.shard_map(body, mesh=mesh, in_specs=in_specs, out_specs=(rows, rows), check_vma=False)
```

```python
import jax
import jax.numpy as jnp
from jax import lax
from jax.experimental import pallas as pl
from jax.experimental.pallas import tpu as pltpu
from jax.sharding import PartitionSpec as P

VMEM = pl.BlockSpec(memory_space=pltpu.VMEM)
HBM = pl.BlockSpec(memory_space=pltpu.HBM)
f32 = jnp.float32
bf16 = jnp.bfloat16


def halves(a):
    hi = a.astype(bf16)
    return hi, (a - hi.astype(f32)).astype(bf16)


def dot(a, b):
    return jnp.dot(a, b, preferred_element_type=f32)


def wide_halves(a):
    return jnp.concatenate(halves(a), axis=1)


def fold(both):
    n = both.shape[1] // 2
    return both[:, :n] + both[:, n:]


def split_product(hi, lo, b_wide):
    n = b_wide.shape[1] // 2
    both = dot(hi, b_wide)
    return both[:, :n] + (both[:, n:] + dot(lo, b_wide[:, :n]))


def product(a, b_wide):
    return split_product(*halves(a), b_wide)


def is_odd():
    return lax.axis_index("wide") % 2 == 1


def send_kernel(x_hbm, v_hbm, rows_hbm, count_hbm, rank_hbm, schur_hbm, u_hbm, near_hbm, rhs_hbm, p_hbm,
                coeff_hbm, a_ref, m_ref, b_ref, sel_ref, x_ref, schur_ref, u_ref, near_ref, rhs_ref, p_ref,
                v_ref, rows_ref, count_ref, rank_ref, coeff_ref, sems, out_sems):
    n_rows, loads = x_ref.shape
    face = rows_ref.shape[2]
    tiles, top, _ = v_ref.shape
    pairs = (
        (x_hbm, x_ref), (rank_hbm, rank_ref), (v_hbm, v_ref), (rows_hbm, rows_ref), (count_hbm, count_ref),
        (schur_hbm, schur_ref), (u_hbm, u_ref), (near_hbm, near_ref), (rhs_hbm, rhs_ref), (p_hbm, p_ref),
    )
    moves = [pltpu.make_async_copy(src, dst, sems.at[i]) for i, (src, dst) in enumerate(pairs)]
    for move in moves:
        move.start()
    moves[0].wait()
    x_wide = wide_halves(x_ref[...])
    for move in moves[1:3]:
        move.wait()
    step = max(1, min(tiles, 256 // top))
    k = lax.broadcasted_iota(jnp.int32, (top, loads), 0)

    def out_move(s):
        span = pl.ds(s * step, step)
        return pltpu.make_async_copy(coeff_ref.at[span], coeff_hbm.at[span], out_sems.at[s])

    for s in range(tiles // step):
        part = v_ref[s * step : (s + 1) * step].reshape(step * top, n_rows)
        out = product(part, x_wide).reshape(step, top, loads)
        for t in range(step):
            coeff_ref[s * step + t] = jnp.where(k < rank_ref[s * step + t], out[t], 0.0)
        out_move(s).start()
    for move in moves[3:5]:
        move.wait()
    odd = is_odd()
    slots = (jnp.where(odd, 0, 2), 1, jnp.where(odd, 2, 0))
    lane = lax.broadcasted_iota(jnp.int32, (1, face), 1)
    across = lax.broadcasted_iota(jnp.int32, (face, n_rows), 1).astype(f32)
    down = lax.broadcasted_iota(jnp.int32, (n_rows, face), 0)
    for spot, out_ref in enumerate((a_ref, m_ref, b_ref)):
        rows = jnp.where(lane < count_ref[slots[spot]], rows_ref[slots[spot]], -1)
        sel_ref[:, spot * face : (spot + 1) * face] = (down == rows).astype(f32).astype(bf16)
        column = jnp.broadcast_to(rows.astype(f32), (face, face)).T[:, :1]
        select = (across == column).astype(f32).astype(bf16)
        out_ref[...] = fold(dot(select, x_wide))
    for s in range(tiles // step):
        out_move(s).wait()
    for move in moves[5:]:
        move.wait()


def place(odd, spot, face):
    if spot == 1:
        return face
    return pl.multiple_of(jnp.where(odd == (spot == 0), 2 * face, 0), face)


def across_kernel(a_ref, m_ref, b_ref, schur_ref, pay_ref, part_ref):
    odd = is_odd()
    face = a_ref.shape[0]
    known = jnp.concatenate([wide_halves(a_ref[...]), wide_halves(m_ref[...])], axis=0)
    pay_ref[:face] = b_ref[...]
    for spot in (2, 0, 1):
        rows = pl.ds(place(odd, spot, face), face)
        block = jnp.concatenate(
            [schur_ref[rows, pl.ds(place(odd, 0, face), face)], schur_ref[rows, face : 2 * face]], axis=1
        )
        out = product(block, known)
        if spot == 2:
            pay_ref[face : 2 * face] = out
            pay_ref[2 * face :] = schur_ref[rows, pl.ds(place(odd, 2, face), face)]
        else:
            part_ref[spot * face : (spot + 1) * face] = out


def base_kernel(rhs_ref, near_ref, x_ref, sel_ref, part_ref, u_ref, p_ref, base_ref, hi_ref, lo_ref, scale_ref):
    n_rows, loads = x_ref.shape
    face = part_ref.shape[0] // 2
    total = rhs_ref[...] - product(near_ref[...], wide_halves(x_ref[...]))
    base_ref[...] = total - fold(dot(sel_ref[:, face : 2 * face], wide_halves(part_ref[face:])))
    hi_ref[...], lo_ref[...] = halves(u_ref[...].T)
    scale_ref[...] = jnp.broadcast_to(p_ref[...], (loads, n_rows)).T


def force_kernel(got_ref, part_ref, schur_ref, _, fa_ref):
    odd = is_odd()
    face = fa_ref.shape[0]
    block = schur_ref[pl.ds(place(odd, 0, face), face), pl.ds(place(odd, 2, face), face)]
    fa_ref[...] = part_ref[:face] + product(block, wide_halves(got_ref[:face]))


def own_kernel(got_ref, out_b_ref, schur_ref, sel_ref, base_ref, next_ref):
    odd = is_odd()
    face = out_b_ref.shape[0]
    block = schur_ref[face : 2 * face, pl.ds(place(odd, 2, face), face)]
    own = product(block, wide_halves(got_ref[:face]))
    back = got_ref[face : 2 * face] + product(got_ref[2 * face :], wide_halves(out_b_ref[...]))
    both = jnp.concatenate([wide_halves(own), wide_halves(back)], axis=0)
    next_ref[...] = base_ref[...] - fold(dot(sel_ref[:, face:], both))


def pair_kernel(back_ref, sel_ref, base_ref, next_ref):
    face = back_ref.shape[0]
    next_ref[...] = base_ref[...] - fold(dot(sel_ref[:, :face], wide_halves(back_ref[...])))


def final_kernel(coeff_ref, hi_ref, lo_ref, base_ref, x_ref, scale_ref, up_ref, res_ref):
    res = base_ref[...] - split_product(hi_ref[...], lo_ref[...], wide_halves(coeff_ref[...]))
    res_ref[...] = res
    up_ref[...] = x_ref[...] + scale_ref[...] * res


def call(kernel, name, outs, operands, in_specs=None, out_specs=None, scratch=(), spaces=None):
    return pl.pallas_call(
        kernel,
        out_shape=tuple(
            space(s, t) for space, (s, t) in zip(spaces or [pltpu.VMEM] * len(outs), outs)
        ),
        in_specs=in_specs or [VMEM] * len(operands),
        out_specs=tuple(out_specs or [VMEM] * len(outs)),
        scratch_shapes=list(scratch),
        compiler_params=pltpu.CompilerParams(vmem_limit_bytes=40 * 2**20),
        name=name,
    )(*operands)


def body(iterate, rhs, schur, near_block, u_basis, v_basis, tile_rank, send_rows, send_count, precond):
    n_rows, loads = iterate.shape
    face = send_rows.shape[2]
    tiles, top, _ = u_basis.shape
    size = lax.axis_size("wide")
    inside = [(i, i ^ 1) for i in range(size) if i ^ 1 < size]
    across = [(i, j) for i in range(size) for j in [i - 1 if i % 2 == 0 else i + 1] if 0 <= j < size]
    schur = schur.reshape(3 * face, 3 * face)
    block = ((face, loads), f32)
    field = ((n_rows, loads), f32)
    factor = ((n_rows, tiles * top), bf16)
    steps = tiles // max(1, min(tiles, 256 // top))

    arrays = (
        iterate,
        v_basis,
        send_rows.reshape(3, 1, face),
        send_count.reshape(3),
        tile_rank.reshape(tiles),
        schur,
        u_basis.reshape(tiles * top, n_rows),
        near_block,
        rhs,
        precond.reshape(1, n_rows),
    )
    square = lambda a: (a.shape, a.dtype)
    coeff, out_a, out_m, out_b, sel, x, schur, u, near, rhs, p = call(
        send_kernel,
        "send",
        [((tiles, top, loads), f32), block, block, block, ((n_rows, 3 * face), bf16), field]
        + [square(arrays[i]) for i in (5, 6, 7, 8, 9)],
        [pltpu.with_memory_space_constraint(a, pltpu.HBM) for a in arrays],
        [HBM] * len(arrays),
        [HBM] + [VMEM] * 10,
        [
            pltpu.VMEM((tiles, top, n_rows), f32),
            pltpu.VMEM((3, 1, face), jnp.int32),
            pltpu.SMEM((3,), jnp.int32),
            pltpu.SMEM((tiles,), jnp.int32),
            pltpu.VMEM((tiles, top, loads), f32),
            pltpu.SemaphoreType.DMA((len(arrays),)),
            pltpu.SemaphoreType.DMA((steps,)),
        ],
        [pltpu.HBM] + [pltpu.VMEM] * 10,
    )
    gathered = lax.all_to_all(coeff, "wide", split_axis=0, concat_axis=0, tiled=True)
    in_a = lax.ppermute(out_a, "wide", inside)
    pay, part = call(
        across_kernel, "across", [((3 * face, loads), f32), ((2 * face, loads), f32)], (in_a, out_m, out_b, schur)
    )
    got = lax.ppermute(pay, "wide", across)
    base, u_hi, u_lo, scale = call(
        base_kernel,
        "base",
        [field, factor, factor, field],
        (rhs, near, x, sel, part, u, p),
    )
    (f_a,) = call(force_kernel, "force", [block], (got, part, schur, base))
    back = lax.ppermute(f_a, "wide", inside)
    (base,) = call(own_kernel, "own", [field], (got, out_b, schur, sel, base))
    (base,) = call(pair_kernel, "pair", [field], (back, sel, base))
    return call(
        final_kernel,
        "final",
        [field, field],
        (gathered.reshape(tiles * top, loads), u_hi, u_lo, base, x, scale),
        spaces=[jax.ShapeDtypeStruct] * 2,
    )


def solution(mesh):
    rows = P(("groups", "wide"), None)
    block = P(("groups", "wide"), None, None)
    basis = P("groups", None, "wide")
    in_specs = (rows, rows, block, rows, basis, basis, P("groups", "wide"), block, rows, P(("groups", "wide")))
    return jax.shard_map(body, mesh=mesh, in_specs=in_specs, out_specs=(rows, rows), check_vma=False)
```

```python
import jax
import jax.numpy as jnp
from jax import lax
from jax.experimental import pallas as pl
from jax.experimental.pallas import tpu as pltpu
from jax.sharding import PartitionSpec as P

VMEM = pl.BlockSpec(memory_space=pltpu.VMEM)
HBM = pl.BlockSpec(memory_space=pltpu.HBM)
f32 = jnp.float32
bf16 = jnp.bfloat16


def halves(a):
    hi = a.astype(bf16)
    return hi, (a - hi.astype(f32)).astype(bf16)


def dot(a, b):
    return jnp.dot(a, b, preferred_element_type=f32)


def wide_halves(a):
    return jnp.concatenate(halves(a), axis=1)


def fold(both):
    n = both.shape[1] // 2
    return both[:, :n] + both[:, n:]


def split_product(hi, lo, b_wide):
    n = b_wide.shape[1] // 2
    both = dot(hi, b_wide)
    return both[:, :n] + (both[:, n:] + dot(lo, b_wide[:, :n]))


def product(a, b_wide):
    return split_product(*halves(a), b_wide)


def is_odd():
    return lax.axis_index("wide") % 2 == 1


def send_kernel(x_hbm, v_hbm, rows_hbm, count_hbm, rank_hbm, schur_hbm, u_hbm, near_hbm, rhs_hbm, p_hbm,
                coeff_hbm, a_ref, m_ref, b_ref, sel_ref, x_ref, schur_ref, u_ref, near_ref, rhs_ref, p_ref,
                v_ref, rows_ref, count_ref, rank_ref, coeff_ref, sems, out_sems):
    n_rows, loads = x_ref.shape
    face = rows_ref.shape[2]
    tiles, top, _ = v_ref.shape
    pairs = (
        (x_hbm, x_ref), (rank_hbm, rank_ref), (v_hbm, v_ref), (rows_hbm, rows_ref), (count_hbm, count_ref),
        (schur_hbm, schur_ref), (u_hbm, u_ref), (near_hbm, near_ref), (rhs_hbm, rhs_ref), (p_hbm, p_ref),
    )
    moves = [pltpu.make_async_copy(src, dst, sems.at[i]) for i, (src, dst) in enumerate(pairs)]
    for move in moves:
        move.start()
    moves[0].wait()
    x_wide = wide_halves(x_ref[...])
    for move in moves[1:3]:
        move.wait()
    step = max(1, min(tiles, 256 // top))
    k = lax.broadcasted_iota(jnp.int32, (top, loads), 0)

    def out_move(s):
        span = pl.ds(s * step, step)
        return pltpu.make_async_copy(coeff_ref.at[span], coeff_hbm.at[span], out_sems.at[s])

    for s in range(tiles // step):
        part = v_ref[s * step : (s + 1) * step].reshape(step * top, n_rows)
        out = product(part, x_wide).reshape(step, top, loads)
        for t in range(step):
            coeff_ref[s * step + t] = jnp.where(k < rank_ref[s * step + t], out[t], 0.0)
        out_move(s).start()
    for move in moves[3:5]:
        move.wait()
    odd = is_odd()
    slots = (jnp.where(odd, 0, 2), 1, jnp.where(odd, 2, 0))
    lane = lax.broadcasted_iota(jnp.int32, (1, face), 1)
    across = lax.broadcasted_iota(jnp.int32, (face, n_rows), 1).astype(f32)
    down = lax.broadcasted_iota(jnp.int32, (n_rows, face), 0)
    for spot, out_ref in enumerate((a_ref, m_ref, b_ref)):
        rows = jnp.where(lane < count_ref[slots[spot]], rows_ref[slots[spot]], -1)
        sel_ref[:, spot * face : (spot + 1) * face] = (down == rows).astype(f32).astype(bf16)
        column = jnp.broadcast_to(rows.astype(f32), (face, face)).T[:, :1]
        select = (across == column).astype(f32).astype(bf16)
        out_ref[...] = fold(dot(select, x_wide))
    for s in range(tiles // step):
        out_move(s).wait()
    for move in moves[5:]:
        move.wait()


def place(odd, spot, face):
    if spot == 1:
        return face
    return pl.multiple_of(jnp.where(odd == (spot == 0), 2 * face, 0), face)


def across_kernel(a_ref, m_ref, b_ref, schur_ref, pay_ref, part_ref):
    odd = is_odd()
    face = a_ref.shape[0]
    known = jnp.concatenate([wide_halves(a_ref[...]), wide_halves(m_ref[...])], axis=0)
    pay_ref[:face] = b_ref[...]
    for spot in (2, 0, 1):
        rows = pl.ds(place(odd, spot, face), face)
        block = jnp.concatenate(
            [schur_ref[rows, pl.ds(place(odd, 0, face), face)], schur_ref[rows, face : 2 * face]], axis=1
        )
        out = product(block, known)
        if spot == 2:
            pay_ref[face : 2 * face] = out
            pay_ref[2 * face :] = schur_ref[rows, pl.ds(place(odd, 2, face), face)]
        else:
            part_ref[spot * face : (spot + 1) * face] = out


def base_kernel(rhs_ref, near_ref, x_ref, sel_ref, part_ref, u_ref, p_ref, base_ref, hi_ref, lo_ref, scale_ref):
    n_rows, loads = x_ref.shape
    face = part_ref.shape[0] // 2
    total = rhs_ref[...] - product(near_ref[...], wide_halves(x_ref[...]))
    base_ref[...] = total - fold(dot(sel_ref[:, face : 2 * face], wide_halves(part_ref[face:])))
    hi_ref[...], lo_ref[...] = halves(u_ref[...].T)
    scale_ref[...] = jnp.broadcast_to(p_ref[...], (loads, n_rows)).T


def force_kernel(got_ref, part_ref, schur_ref, _, fa_ref):
    odd = is_odd()
    face = fa_ref.shape[0]
    block = schur_ref[pl.ds(place(odd, 0, face), face), pl.ds(place(odd, 2, face), face)]
    fa_ref[...] = part_ref[:face] + product(block, wide_halves(got_ref[:face]))


def own_kernel(got_ref, out_b_ref, schur_ref, sel_ref, base_ref, next_ref):
    odd = is_odd()
    face = out_b_ref.shape[0]
    block = schur_ref[face : 2 * face, pl.ds(place(odd, 2, face), face)]
    own = product(block, wide_halves(got_ref[:face]))
    back = got_ref[face : 2 * face] + product(got_ref[2 * face :], wide_halves(out_b_ref[...]))
    both = jnp.concatenate([wide_halves(own), wide_halves(back)], axis=0)
    next_ref[...] = base_ref[...] - fold(dot(sel_ref[:, face:], both))


def far_kernel(coeff_ref, hi_ref, lo_ref, base_ref, next_ref):
    next_ref[...] = base_ref[...] - split_product(hi_ref[...], lo_ref[...], wide_halves(coeff_ref[...]))


def final_kernel(back_ref, sel_ref, base_ref, x_ref, scale_ref, up_ref, res_ref):
    face = back_ref.shape[0]
    res = base_ref[...] - fold(dot(sel_ref[:, :face], wide_halves(back_ref[...])))
    res_ref[...] = res
    up_ref[...] = x_ref[...] + scale_ref[...] * res


def call(kernel, name, outs, operands, in_specs=None, out_specs=None, scratch=(), spaces=None, cost=0):
    return pl.pallas_call(
        kernel,
        out_shape=tuple(
            space(s, t) for space, (s, t) in zip(spaces or [pltpu.VMEM] * len(outs), outs)
        ),
        in_specs=in_specs or [VMEM] * len(operands),
        out_specs=tuple(out_specs or [VMEM] * len(outs)),
        scratch_shapes=list(scratch),
        compiler_params=pltpu.CompilerParams(vmem_limit_bytes=40 * 2**20),
        cost_estimate=pl.CostEstimate(flops=cost, bytes_accessed=0, transcendentals=0) if cost else None,
        name=name,
    )(*operands)


def body(iterate, rhs, schur, near_block, u_basis, v_basis, tile_rank, send_rows, send_count, precond):
    n_rows, loads = iterate.shape
    face = send_rows.shape[2]
    tiles, top, _ = u_basis.shape
    size = lax.axis_size("wide")
    inside = [(i, i ^ 1) for i in range(size) if i ^ 1 < size]
    across = [(i, j) for i in range(size) for j in [i - 1 if i % 2 == 0 else i + 1] if 0 <= j < size]
    schur = schur.reshape(3 * face, 3 * face)
    block = ((face, loads), f32)
    field = ((n_rows, loads), f32)
    factor = ((n_rows, tiles * top), bf16)
    steps = tiles // max(1, min(tiles, 256 // top))

    arrays = (
        iterate,
        v_basis,
        send_rows.reshape(3, 1, face),
        send_count.reshape(3),
        tile_rank.reshape(tiles),
        schur,
        u_basis.reshape(tiles * top, n_rows),
        near_block,
        rhs,
        precond.reshape(1, n_rows),
    )
    square = lambda a: (a.shape, a.dtype)
    coeff, out_a, out_m, out_b, sel, x, schur, u, near, rhs, p = call(
        send_kernel,
        "send",
        [((tiles, top, loads), f32), block, block, block, ((n_rows, 3 * face), bf16), field]
        + [square(arrays[i]) for i in (5, 6, 7, 8, 9)],
        [pltpu.with_memory_space_constraint(a, pltpu.HBM) for a in arrays],
        [HBM] * len(arrays),
        [HBM] + [VMEM] * 10,
        [
            pltpu.VMEM((tiles, top, n_rows), f32),
            pltpu.VMEM((3, 1, face), jnp.int32),
            pltpu.SMEM((3,), jnp.int32),
            pltpu.SMEM((tiles,), jnp.int32),
            pltpu.VMEM((tiles, top, loads), f32),
            pltpu.SemaphoreType.DMA((len(arrays),)),
            pltpu.SemaphoreType.DMA((steps,)),
        ],
        [pltpu.HBM] + [pltpu.VMEM] * 10,
    )
    gathered = lax.all_to_all(coeff, "wide", split_axis=0, concat_axis=0, tiled=True)
    in_a = lax.ppermute(out_a, "wide", inside)
    pay, part = call(
        across_kernel, "across", [((3 * face, loads), f32), ((2 * face, loads), f32)], (in_a, out_m, out_b, schur), cost=10000000000
    )
    got = lax.ppermute(pay, "wide", across)
    base, u_hi, u_lo, scale = call(
        base_kernel,
        "base",
        [field, factor, factor, field],
        (rhs, near, x, sel, part, u, p),
    )
    (f_a,) = call(force_kernel, "force", [block], (got, part, schur, base), cost=0)
    back = lax.ppermute(f_a, "wide", inside)
    (base,) = call(own_kernel, "own", [field], (got, out_b, schur, sel, base))
    (base,) = call(far_kernel, "far", [field], (gathered.reshape(tiles * top, loads), u_hi, u_lo, base))
    return call(
        final_kernel, "final", [field, field], (back, sel, base, x, scale), spaces=[jax.ShapeDtypeStruct] * 2
    )


def solution(mesh):
    rows = P(("groups", "wide"), None)
    block = P(("groups", "wide"), None, None)
    basis = P("groups", None, "wide")
    in_specs = (rows, rows, block, rows, basis, basis, P("groups", "wide"), block, rows, P(("groups", "wide")))
    return jax.shard_map(body, mesh=mesh, in_specs=in_specs, out_specs=(rows, rows), check_vma=False)
```

```python
import jax
import jax.numpy as jnp
from jax import lax
from jax.experimental import pallas as pl
from jax.experimental.pallas import tpu as pltpu
from jax.sharding import PartitionSpec as P

VMEM = pl.BlockSpec(memory_space=pltpu.VMEM)
HBM = pl.BlockSpec(memory_space=pltpu.HBM)
f32 = jnp.float32
bf16 = jnp.bfloat16


def halves(a):
    hi = a.astype(bf16)
    return hi, (a - hi.astype(f32)).astype(bf16)


def dot(a, b):
    return jnp.dot(a, b, preferred_element_type=f32)


def wide_halves(a):
    return jnp.concatenate(halves(a), axis=1)


def fold(both):
    n = both.shape[1] // 2
    return both[:, :n] + both[:, n:]


def split_product(hi, lo, b_wide):
    n = b_wide.shape[1] // 2
    both = dot(hi, b_wide)
    return both[:, :n] + (both[:, n:] + dot(lo, b_wide[:, :n]))


def product(a, b_wide):
    return split_product(*halves(a), b_wide)


def is_odd():
    return lax.axis_index("wide") % 2 == 1


def send_kernel(x_hbm, v_hbm, rows_hbm, count_hbm, rank_hbm, schur_hbm, u_hbm, near_hbm, rhs_hbm, p_hbm,
                coeff_hbm, a_ref, m_ref, b_ref, sel_ref, x_ref, schur_ref, u_ref, near_ref, rhs_ref, p_ref,
                v_ref, rows_ref, count_ref, rank_ref, coeff_ref, sems, out_sems):
    n_rows, loads = x_ref.shape
    face = rows_ref.shape[2]
    tiles, top, _ = v_ref.shape
    pairs = (
        (x_hbm, x_ref), (rank_hbm, rank_ref), (v_hbm, v_ref), (rows_hbm, rows_ref), (count_hbm, count_ref),
        (schur_hbm, schur_ref), (u_hbm, u_ref), (near_hbm, near_ref), (rhs_hbm, rhs_ref), (p_hbm, p_ref),
    )
    moves = [pltpu.make_async_copy(src, dst, sems.at[i]) for i, (src, dst) in enumerate(pairs)]
    for move in moves:
        move.start()
    moves[0].wait()
    x_wide = wide_halves(x_ref[...])
    for move in moves[1:3]:
        move.wait()
    step = max(1, min(tiles, 256 // top))
    k = lax.broadcasted_iota(jnp.int32, (top, loads), 0)

    def out_move(s):
        span = pl.ds(s * step, step)
        return pltpu.make_async_copy(coeff_ref.at[span], coeff_hbm.at[span], out_sems.at[s])

    for s in range(tiles // step):
        part = v_ref[s * step : (s + 1) * step].reshape(step * top, n_rows)
        out = product(part, x_wide).reshape(step, top, loads)
        for t in range(step):
            coeff_ref[s * step + t] = jnp.where(k < rank_ref[s * step + t], out[t], 0.0)
        out_move(s).start()
    for move in moves[3:5]:
        move.wait()
    odd = is_odd()
    slots = (jnp.where(odd, 0, 2), 1, jnp.where(odd, 2, 0))
    lane = lax.broadcasted_iota(jnp.int32, (1, face), 1)
    across = lax.broadcasted_iota(jnp.int32, (face, n_rows), 1).astype(f32)
    down = lax.broadcasted_iota(jnp.int32, (n_rows, face), 0)
    for spot, out_ref in enumerate((a_ref, m_ref, b_ref)):
        rows = jnp.where(lane < count_ref[slots[spot]], rows_ref[slots[spot]], -1)
        sel_ref[:, spot * face : (spot + 1) * face] = (down == rows).astype(f32).astype(bf16)
        column = jnp.broadcast_to(rows.astype(f32), (face, face)).T[:, :1]
        select = (across == column).astype(f32).astype(bf16)
        out_ref[...] = fold(dot(select, x_wide))
    for s in range(tiles // step):
        out_move(s).wait()
    for move in moves[5:]:
        move.wait()


def place(odd, spot, face):
    if spot == 1:
        return face
    return pl.multiple_of(jnp.where(odd == (spot == 0), 2 * face, 0), face)


def across_kernel(a_ref, m_ref, b_ref, schur_ref, pay_ref, part_ref):
    odd = is_odd()
    face = a_ref.shape[0]
    known = jnp.concatenate([wide_halves(a_ref[...]), wide_halves(m_ref[...])], axis=0)
    pay_ref[:face] = b_ref[...]
    for spot in (2, 0, 1):
        rows = pl.ds(place(odd, spot, face), face)
        block = jnp.concatenate(
            [schur_ref[rows, pl.ds(place(odd, 0, face), face)], schur_ref[rows, face : 2 * face]], axis=1
        )
        out = product(block, known)
        if spot == 2:
            pay_ref[face : 2 * face] = out
            pay_ref[2 * face :] = schur_ref[rows, pl.ds(place(odd, 2, face), face)]
        else:
            part_ref[spot * face : (spot + 1) * face] = out


def force_kernel(got_ref, part_ref, schur_ref, fa_ref):
    odd = is_odd()
    face = fa_ref.shape[0]
    got_ref = got_ref.at[odd.astype(jnp.int32)]
    block = schur_ref[pl.ds(place(odd, 0, face), face), pl.ds(place(odd, 2, face), face)]
    fa_ref[...] = part_ref[:face] + product(block, wide_halves(got_ref[:face]))


def local_kernel(got_ref, part_ref, out_b_ref, schur_ref, sel_ref, rhs_ref, near_ref, x_ref, u_ref, p_ref,
                 base_ref, hi_ref, lo_ref, scale_ref):
    odd = is_odd()
    n_rows, loads = x_ref.shape
    face = out_b_ref.shape[0]
    got_ref = got_ref.at[odd.astype(jnp.int32)]
    block = schur_ref[face : 2 * face, pl.ds(place(odd, 2, face), face)]
    own = part_ref[face:] + product(block, wide_halves(got_ref[:face]))
    back = got_ref[face : 2 * face] + product(got_ref[2 * face :], wide_halves(out_b_ref[...]))
    both = jnp.concatenate([wide_halves(own), wide_halves(back)], axis=0)
    near = product(near_ref[...], wide_halves(x_ref[...]))
    base_ref[...] = rhs_ref[...] - near - fold(dot(sel_ref[:, face:], both))
    hi_ref[...], lo_ref[...] = halves(u_ref[...].T)
    scale_ref[...] = jnp.broadcast_to(p_ref[...], (loads, n_rows)).T


def far_kernel(coeff_ref, hi_ref, lo_ref, base_ref, next_ref):
    next_ref[...] = base_ref[...] - split_product(hi_ref[...], lo_ref[...], wide_halves(coeff_ref[...]))


def final_kernel(back_ref, sel_ref, base_ref, x_ref, scale_ref, up_ref, res_ref):
    face = back_ref.shape[0]
    res = base_ref[...] - fold(dot(sel_ref[:, :face], wide_halves(back_ref[...])))
    res_ref[...] = res
    up_ref[...] = x_ref[...] + scale_ref[...] * res


def call(kernel, name, outs, operands, in_specs=None, out_specs=None, scratch=(), spaces=None, cost=0):
    return pl.pallas_call(
        kernel,
        out_shape=tuple(
            space(s, t) for space, (s, t) in zip(spaces or [pltpu.VMEM] * len(outs), outs)
        ),
        in_specs=in_specs or [VMEM] * len(operands),
        out_specs=tuple(out_specs or [VMEM] * len(outs)),
        scratch_shapes=list(scratch),
        compiler_params=pltpu.CompilerParams(vmem_limit_bytes=40 * 2**20),
        cost_estimate=pl.CostEstimate(flops=cost, bytes_accessed=0, transcendentals=0) if cost else None,
        name=name,
    )(*operands)


def body(iterate, rhs, schur, near_block, u_basis, v_basis, tile_rank, send_rows, send_count, precond):
    n_rows, loads = iterate.shape
    face = send_rows.shape[2]
    tiles, top, _ = u_basis.shape
    size = lax.axis_size("wide")
    parts = lax.axis_size("groups")
    inside = [(i, i ^ 1) for i in range(size) if i ^ 1 < size]
    across = [[g * size + i - 1, g * size + i] for g in range(parts) for i in range(2, size, 2)]
    for g in range(0, parts, 2):
        across += [[g * size + size - 1, (g + 1) * size + size - 1], [(g + 1) * size, g * size]]
    schur = schur.reshape(3 * face, 3 * face)
    block = ((face, loads), f32)
    field = ((n_rows, loads), f32)
    factor = ((n_rows, tiles * top), bf16)
    steps = tiles // max(1, min(tiles, 256 // top))

    arrays = (
        iterate,
        v_basis,
        send_rows.reshape(3, 1, face),
        send_count.reshape(3),
        tile_rank.reshape(tiles),
        schur,
        u_basis.reshape(tiles * top, n_rows),
        near_block,
        rhs,
        precond.reshape(1, n_rows),
    )
    square = lambda a: (a.shape, a.dtype)
    coeff, out_a, out_m, out_b, sel, x, schur, u, near, rhs, p = call(
        send_kernel,
        "send",
        [((tiles, top, loads), f32), block, block, block, ((n_rows, 3 * face), bf16), field]
        + [square(arrays[i]) for i in (5, 6, 7, 8, 9)],
        [pltpu.with_memory_space_constraint(a, pltpu.HBM) for a in arrays],
        [HBM] * len(arrays),
        [HBM] + [VMEM] * 10,
        [
            pltpu.VMEM((tiles, top, n_rows), f32),
            pltpu.VMEM((3, 1, face), jnp.int32),
            pltpu.SMEM((3,), jnp.int32),
            pltpu.SMEM((tiles,), jnp.int32),
            pltpu.VMEM((tiles, top, loads), f32),
            pltpu.SemaphoreType.DMA((len(arrays),)),
            pltpu.SemaphoreType.DMA((steps,)),
        ],
        [pltpu.HBM] + [pltpu.VMEM] * 10,
    )
    gathered = lax.all_to_all(coeff, "wide", split_axis=0, concat_axis=0, tiled=True)
    in_a = lax.ppermute(out_a, "wide", inside)
    pay, part = call(
        across_kernel, "across", [((3 * face, loads), f32), ((2 * face, loads), f32)], (in_a, out_m, out_b, schur), cost=10000000000
    )
    got = lax.all_gather(pay, ("groups", "wide"), axis_index_groups=across)
    (f_a,) = call(force_kernel, "force", [block], (got, part, schur))
    back = lax.ppermute(f_a, "wide", inside)
    base, u_hi, u_lo, scale = call(
        local_kernel,
        "local",
        [field, factor, factor, field],
        (got, part, out_b, schur, sel, rhs, near, x, u, p),
    )
    (base,) = call(far_kernel, "far", [field], (gathered.reshape(tiles * top, loads), u_hi, u_lo, base))
    return call(
        final_kernel, "final", [field, field], (back, sel, base, x, scale), spaces=[jax.ShapeDtypeStruct] * 2
    )


def solution(mesh):
    rows = P(("groups", "wide"), None)
    block = P(("groups", "wide"), None, None)
    basis = P("groups", None, "wide")
    in_specs = (rows, rows, block, rows, basis, basis, P("groups", "wide"), block, rows, P(("groups", "wide")))
    return jax.shard_map(body, mesh=mesh, in_specs=in_specs, out_specs=(rows, rows), check_vma=False)
```

```python
import math

import jax
import jax.numpy as jnp
from jax import lax
from jax.experimental import pallas as pl
from jax.experimental.pallas import tpu as pltpu
from jax.sharding import PartitionSpec as P

VMEM = pl.BlockSpec(memory_space=pltpu.VMEM)
HBM = pl.BlockSpec(memory_space=pltpu.HBM)
f32 = jnp.float32
bf16 = jnp.bfloat16


def halves(a):
    hi = a.astype(bf16)
    return hi, (a - hi.astype(f32)).astype(bf16)


def dot(a, b):
    return jnp.dot(a, b, preferred_element_type=f32)


def wide_halves(a):
    return jnp.concatenate(halves(a), axis=1)


def fold(both):
    n = both.shape[1] // 2
    return both[:, :n] + both[:, n:]


def split_product(hi, lo, b_wide):
    n = b_wide.shape[1] // 2
    both = dot(hi, b_wide)
    return both[:, :n] + (both[:, n:] + dot(lo, b_wide[:, :n]))


def product(a, b_wide):
    return split_product(*halves(a), b_wide)


def is_odd():
    return lax.axis_index("wide") % 2 == 1


def tiles_at_once(tiles, top):
    return math.gcd(tiles, max(1, 256 // top))


def send_kernel(x_hbm, v_hbm, rows_hbm, count_hbm, rank_hbm, schur_hbm, u_hbm, near_hbm, rhs_hbm, p_hbm,
                coeff_hbm, a_ref, m_ref, b_ref, sel_ref, x_ref, schur_ref, u_ref, near_ref, rhs_ref, p_ref,
                v_ref, rows_ref, count_ref, rank_ref, coeff_ref, sems, out_sems):
    n_rows, loads = x_ref.shape
    face = rows_ref.shape[2]
    tiles, top, _ = v_ref.shape
    pairs = (
        (x_hbm, x_ref), (rank_hbm, rank_ref), (v_hbm, v_ref), (rows_hbm, rows_ref), (count_hbm, count_ref),
        (schur_hbm, schur_ref), (u_hbm, u_ref), (near_hbm, near_ref), (rhs_hbm, rhs_ref), (p_hbm, p_ref),
    )
    moves = [pltpu.make_async_copy(src, dst, sems.at[i]) for i, (src, dst) in enumerate(pairs)]
    for move in moves:
        move.start()
    moves[0].wait()
    x_wide = wide_halves(x_ref[...])
    for move in moves[1:3]:
        move.wait()
    step = tiles_at_once(tiles, top)
    k = lax.broadcasted_iota(jnp.int32, (top, loads), 0)

    def out_move(s):
        span = pl.ds(s * step, step)
        return pltpu.make_async_copy(coeff_ref.at[span], coeff_hbm.at[span], out_sems.at[s])

    for s in range(tiles // step):
        part = v_ref[s * step : (s + 1) * step].reshape(step * top, n_rows)
        out = product(part, x_wide).reshape(step, top, loads)
        for t in range(step):
            coeff_ref[s * step + t] = jnp.where(k < rank_ref[s * step + t], out[t], 0.0)
        out_move(s).start()
    for move in moves[3:5]:
        move.wait()
    odd = is_odd()
    slots = (jnp.where(odd, 0, 2), 1, jnp.where(odd, 2, 0))
    lane = lax.broadcasted_iota(jnp.int32, (1, face), 1)
    across = lax.broadcasted_iota(jnp.int32, (face, n_rows), 1).astype(f32)
    down = lax.broadcasted_iota(jnp.int32, (n_rows, face), 0)
    for spot, out_ref in enumerate((a_ref, m_ref, b_ref)):
        rows = jnp.where(lane < count_ref[slots[spot]], rows_ref[slots[spot]], -1)
        sel_ref[:, spot * face : (spot + 1) * face] = (down == rows).astype(f32).astype(bf16)
        column = jnp.broadcast_to(rows.astype(f32), (face, face)).T[:, :1]
        select = (across == column).astype(f32).astype(bf16)
        out_ref[...] = fold(dot(select, x_wide))
    for s in range(tiles // step):
        out_move(s).wait()
    for move in moves[5:]:
        move.wait()


def place(odd, spot, face):
    if spot == 1:
        return face
    return pl.multiple_of(jnp.where(odd == (spot == 0), 2 * face, 0), face)


def across_kernel(a_ref, m_ref, schur_ref, pay_ref, part_ref):
    odd = is_odd()
    face = a_ref.shape[0]
    last = pl.ds(place(odd, 2, face), face)
    known = jnp.concatenate([wide_halves(a_ref[...]), wide_halves(m_ref[...])], axis=0)
    pay_ref[face:] = schur_ref[last, last]
    for spot in (2, 0, 1):
        rows = pl.ds(place(odd, spot, face), face)
        block = jnp.concatenate(
            [schur_ref[rows, pl.ds(place(odd, 0, face), face)], schur_ref[rows, face : 2 * face]], axis=1
        )
        out = product(block, known)
        if spot == 2:
            pay_ref[:face] = out
        else:
            part_ref[spot * face : (spot + 1) * face] = out


def base_kernel(rhs_ref, near_ref, x_ref, u_ref, p_ref, _, base_ref, hi_ref, lo_ref, scale_ref):
    n_rows, loads = x_ref.shape
    base_ref[...] = rhs_ref[...] - product(near_ref[...], wide_halves(x_ref[...]))
    hi_ref[...], lo_ref[...] = halves(u_ref[...].T)
    scale_ref[...] = jnp.broadcast_to(p_ref[...], (loads, n_rows)).T


def force_kernel(got_ref, part_ref, schur_ref, fa_ref):
    odd = is_odd()
    face = fa_ref.shape[0]
    block = schur_ref[pl.ds(place(odd, 0, face), face), pl.ds(place(odd, 2, face), face)]
    fa_ref[...] = part_ref[:face] + product(block, wide_halves(got_ref[...]))


def own_kernel(got_ref, part_ref, schur_ref, sel_ref, base_ref, next_ref):
    odd = is_odd()
    face = got_ref.shape[0]
    block = schur_ref[face : 2 * face, pl.ds(place(odd, 2, face), face)]
    own = part_ref[face:] + product(block, wide_halves(got_ref[...]))
    next_ref[...] = base_ref[...] - fold(dot(sel_ref[:, face : 2 * face], wide_halves(own)))


def back_kernel(pay_ref, out_b_ref, back_ref, sel_ref, base_ref, next_ref):
    face = back_ref.shape[0]
    b = pay_ref[:face] + product(pay_ref[face:], wide_halves(out_b_ref[...]))
    a = dot(sel_ref[:, :face], wide_halves(back_ref[...]))
    b = dot(sel_ref[:, 2 * face :], wide_halves(b))
    next_ref[...] = base_ref[...] - fold(a + b)


def final_kernel(coeff_ref, hi_ref, lo_ref, base_ref, x_ref, scale_ref, up_ref, res_ref):
    res = base_ref[...] - split_product(hi_ref[...], lo_ref[...], wide_halves(coeff_ref[...]))
    res_ref[...] = res
    up_ref[...] = x_ref[...] + scale_ref[...] * res


def call(kernel, name, outs, operands, in_specs=None, out_specs=None, scratch=(), spaces=None):
    return pl.pallas_call(
        kernel,
        out_shape=tuple(
            space(s, t) for space, (s, t) in zip(spaces or [pltpu.VMEM] * len(outs), outs)
        ),
        in_specs=in_specs or [VMEM] * len(operands),
        out_specs=tuple(out_specs or [VMEM] * len(outs)),
        scratch_shapes=list(scratch),
        compiler_params=pltpu.CompilerParams(vmem_limit_bytes=40 * 2**20),
        name=name,
    )(*operands)


def body(iterate, rhs, schur, near_block, u_basis, v_basis, tile_rank, send_rows, send_count, precond):
    n_rows, loads = iterate.shape
    face = send_rows.shape[2]
    tiles, top, _ = u_basis.shape
    size = lax.axis_size("wide")
    parts = lax.axis_size("groups")
    inside = [(i, i ^ 1) for i in range(size) if i ^ 1 < size]
    across = [(g * size + i, g * size + (i - 1 if i % 2 == 0 else i + 1)) for g in range(parts) for i in range(1, size - 1)]
    across += [(g * size + i, (g + 1) % parts * size + i) for g in range(parts) for i in (0, size - 1)]
    schur = schur.reshape(3 * face, 3 * face)
    block = ((face, loads), f32)
    field = ((n_rows, loads), f32)
    factor = ((n_rows, tiles * top), bf16)
    steps = tiles // tiles_at_once(tiles, top)

    arrays = (
        iterate,
        v_basis,
        send_rows.reshape(3, 1, face),
        send_count.reshape(3),
        tile_rank.reshape(tiles),
        schur,
        u_basis.reshape(tiles * top, n_rows),
        near_block,
        rhs,
        precond.reshape(1, n_rows),
    )
    square = lambda a: (a.shape, a.dtype)
    coeff, out_a, out_m, out_b, sel, x, schur, u, near, rhs, p = call(
        send_kernel,
        "send",
        [((tiles, top, loads), f32), block, block, block, ((n_rows, 3 * face), bf16), field]
        + [square(arrays[i]) for i in (5, 6, 7, 8, 9)],
        [pltpu.with_memory_space_constraint(a, pltpu.HBM) for a in arrays],
        [HBM] * len(arrays),
        [HBM] + [VMEM] * 10,
        [
            pltpu.VMEM((tiles, top, n_rows), f32),
            pltpu.VMEM((3, 1, face), jnp.int32),
            pltpu.SMEM((3,), jnp.int32),
            pltpu.SMEM((tiles,), jnp.int32),
            pltpu.VMEM((tiles, top, loads), f32),
            pltpu.SemaphoreType.DMA((len(arrays),)),
            pltpu.SemaphoreType.DMA((steps,)),
        ],
        [pltpu.HBM] + [pltpu.VMEM] * 10,
    )
    gathered = lax.all_to_all(coeff, "wide", split_axis=0, concat_axis=0, tiled=True)
    in_a = lax.ppermute(out_a, "wide", inside)
    got = lax.ppermute(out_b, ("groups", "wide"), across)
    pay, part = call(
        across_kernel, "across", [((2 * face, loads), f32)] * 2, (in_a, out_m, schur)
    )
    sums = lax.ppermute(pay, ("groups", "wide"), across)
    base, u_hi, u_lo, scale = call(
        base_kernel, "base", [field, factor, factor, field], (rhs, near, x, u, p, part)
    )
    (f_a,) = call(force_kernel, "force", [block], (got, part, schur))
    back = lax.ppermute(f_a, "wide", inside)
    (base,) = call(own_kernel, "own", [field], (got, part, schur, sel, base))
    (base,) = call(back_kernel, "back", [field], (sums, out_b, back, sel, base))
    return call(
        final_kernel,
        "final",
        [field, field],
        (gathered.reshape(tiles * top, loads), u_hi, u_lo, base, x, scale),
        spaces=[jax.ShapeDtypeStruct] * 2,
    )


def solution(mesh):
    rows = P(("groups", "wide"), None)
    block = P(("groups", "wide"), None, None)
    basis = P("groups", None, "wide")
    in_specs = (rows, rows, block, rows, basis, basis, P("groups", "wide"), block, rows, P(("groups", "wide")))
    return jax.shard_map(body, mesh=mesh, in_specs=in_specs, out_specs=(rows, rows), check_vma=False)
```

```python
import math

import jax
import jax.numpy as jnp
from jax import lax
from jax.experimental import pallas as pl
from jax.experimental.pallas import tpu as pltpu
from jax.sharding import PartitionSpec as P

VMEM = pl.BlockSpec(memory_space=pltpu.VMEM)
HBM = pl.BlockSpec(memory_space=pltpu.HBM)
f32 = jnp.float32
bf16 = jnp.bfloat16


def halves(a):
    hi = a.astype(bf16)
    return hi, (a - hi.astype(f32)).astype(bf16)


def dot(a, b):
    return jnp.dot(a, b, preferred_element_type=f32)


def wide_halves(a):
    return jnp.concatenate(halves(a), axis=1)


def fold(both):
    n = both.shape[1] // 2
    return both[:, :n] + both[:, n:]


def split_product(hi, lo, b_wide):
    n = b_wide.shape[1] // 2
    both = dot(hi, b_wide)
    return both[:, :n] + (both[:, n:] + dot(lo, b_wide[:, :n]))


def product(a, b_wide):
    return split_product(*halves(a), b_wide)


def is_odd():
    return lax.axis_index("wide") % 2 == 1


def lead(size):
    pairs = size // 2
    return (2 * (pairs // 2 + math.isqrt(pairs) // 2) + 1) % size


def turned(hbm, ref, by):
    rest = hbm.shape[0] - by
    if by == 0:
        return [(hbm, ref)]
    return [(hbm.at[pl.ds(by, rest)], ref.at[pl.ds(0, rest)]), (hbm.at[pl.ds(0, by)], ref.at[pl.ds(rest, by)])]


def tiles_at_once(tiles, top):
    return math.gcd(tiles, max(1, 256 // top))


def send_kernel(x_hbm, v_hbm, rows_hbm, count_hbm, rank_hbm, schur_hbm, u_hbm, near_hbm, rhs_hbm, p_hbm,
                coeff_hbm, a_ref, m_ref, b_ref, sel_ref, x_ref, schur_ref, u_ref, near_ref, rhs_ref, p_ref,
                v_ref, rows_ref, count_ref, rank_ref, coeff_ref, sems, out_sems):
    n_rows, loads = x_ref.shape
    face = rows_ref.shape[2]
    tiles, top, _ = v_ref.shape
    first = lead(tiles)
    early = [(x_hbm, x_ref), (rank_hbm, rank_ref)] + turned(v_hbm, v_ref, first)
    middle = [(rows_hbm, rows_ref), (count_hbm, count_ref)]
    late = [(schur_hbm, schur_ref)] + turned(u_hbm, u_ref, first * top)
    late += [(near_hbm, near_ref), (rhs_hbm, rhs_ref), (p_hbm, p_ref)]
    moves = [pltpu.make_async_copy(src, dst, sems.at[i]) for i, (src, dst) in enumerate(early + middle + late)]
    for move in moves:
        move.start()
    moves[0].wait()
    x_wide = wide_halves(x_ref[...])
    for move in moves[1 : len(early)]:
        move.wait()
    step = tiles_at_once(tiles, top)
    k = lax.broadcasted_iota(jnp.int32, (top, loads), 0)

    def out_move(s):
        span = pl.ds(s * step, step)
        return pltpu.make_async_copy(coeff_ref.at[span], coeff_hbm.at[span], out_sems.at[s])

    for s in range(tiles // step):
        part = v_ref[s * step : (s + 1) * step].reshape(step * top, n_rows)
        out = product(part, x_wide).reshape(step, top, loads)
        for t in range(step):
            at = s * step + t
            coeff_ref[at] = jnp.where(k < rank_ref[(at + first) % tiles], out[t], 0.0)
        out_move(s).start()
    for move in moves[len(early) : -len(late)]:
        move.wait()
    odd = is_odd()
    slots = (jnp.where(odd, 0, 2), 1, jnp.where(odd, 2, 0))
    lane = lax.broadcasted_iota(jnp.int32, (1, face), 1)
    across = lax.broadcasted_iota(jnp.int32, (face, n_rows), 1).astype(f32)
    down = lax.broadcasted_iota(jnp.int32, (n_rows, face), 0)
    for spot, out_ref in enumerate((a_ref, m_ref, b_ref)):
        rows = jnp.where(lane < count_ref[slots[spot]], rows_ref[slots[spot]], -1)
        sel_ref[:, spot * face : (spot + 1) * face] = (down == rows).astype(f32).astype(bf16)
        column = jnp.broadcast_to(rows.astype(f32), (face, face)).T[:, :1]
        select = (across == column).astype(f32).astype(bf16)
        out_ref[...] = fold(dot(select, x_wide))
    for s in range(tiles // step):
        out_move(s).wait()
    for move in moves[-len(late) :]:
        move.wait()


def place(odd, spot, face):
    if spot == 1:
        return face
    return pl.multiple_of(jnp.where(odd == (spot == 0), 2 * face, 0), face)


def across_kernel(a_ref, m_ref, schur_ref, pay_ref, part_ref):
    odd = is_odd()
    face = a_ref.shape[0]
    last = pl.ds(place(odd, 2, face), face)
    known = jnp.concatenate([wide_halves(a_ref[...]), wide_halves(m_ref[...])], axis=0)
    pay_ref[face:] = schur_ref[last, last]
    for spot in (2, 0, 1):
        rows = pl.ds(place(odd, spot, face), face)
        block = jnp.concatenate(
            [schur_ref[rows, pl.ds(place(odd, 0, face), face)], schur_ref[rows, face : 2 * face]], axis=1
        )
        out = product(block, known)
        if spot == 2:
            pay_ref[:face] = out
        else:
            part_ref[spot * face : (spot + 1) * face] = out


def base_kernel(rhs_ref, near_ref, x_ref, u_ref, p_ref, _, base_ref, hi_ref, lo_ref, scale_ref):
    n_rows, loads = x_ref.shape
    base_ref[...] = rhs_ref[...] - product(near_ref[...], wide_halves(x_ref[...]))
    hi_ref[...], lo_ref[...] = halves(u_ref[...].T)
    scale_ref[...] = jnp.broadcast_to(p_ref[...], (loads, n_rows)).T


def force_kernel(got_ref, part_ref, schur_ref, fa_ref):
    odd = is_odd()
    face = fa_ref.shape[0]
    block = schur_ref[pl.ds(place(odd, 0, face), face), pl.ds(place(odd, 2, face), face)]
    fa_ref[...] = part_ref[:face] + product(block, wide_halves(got_ref[...]))


def own_kernel(got_ref, part_ref, schur_ref, sel_ref, base_ref, next_ref):
    odd = is_odd()
    face = got_ref.shape[0]
    block = schur_ref[face : 2 * face, pl.ds(place(odd, 2, face), face)]
    own = part_ref[face:] + product(block, wide_halves(got_ref[...]))
    next_ref[...] = base_ref[...] - fold(dot(sel_ref[:, face : 2 * face], wide_halves(own)))


def back_kernel(pay_ref, out_b_ref, back_ref, sel_ref, base_ref, next_ref):
    face = back_ref.shape[0]
    b = pay_ref[:face] + product(pay_ref[face:], wide_halves(out_b_ref[...]))
    a = dot(sel_ref[:, :face], wide_halves(back_ref[...]))
    b = dot(sel_ref[:, 2 * face :], wide_halves(b))
    next_ref[...] = base_ref[...] - fold(a + b)


def final_kernel(coeff_ref, hi_ref, lo_ref, base_ref, x_ref, scale_ref, up_ref, res_ref):
    res = base_ref[...] - split_product(hi_ref[...], lo_ref[...], wide_halves(coeff_ref[...]))
    res_ref[...] = res
    up_ref[...] = x_ref[...] + scale_ref[...] * res


def call(kernel, name, outs, operands, in_specs=None, out_specs=None, scratch=(), spaces=None):
    return pl.pallas_call(
        kernel,
        out_shape=tuple(
            space(s, t) for space, (s, t) in zip(spaces or [pltpu.VMEM] * len(outs), outs)
        ),
        in_specs=in_specs or [VMEM] * len(operands),
        out_specs=tuple(out_specs or [VMEM] * len(outs)),
        scratch_shapes=list(scratch),
        compiler_params=pltpu.CompilerParams(vmem_limit_bytes=40 * 2**20),
        name=name,
    )(*operands)


def body(iterate, rhs, schur, near_block, u_basis, v_basis, tile_rank, send_rows, send_count, precond):
    n_rows, loads = iterate.shape
    face = send_rows.shape[2]
    tiles, top, _ = u_basis.shape
    size = lax.axis_size("wide")
    parts = lax.axis_size("groups")
    inside = [(i, i ^ 1) for i in range(size) if i ^ 1 < size]
    across = [(g * size + i, g * size + (i - 1 if i % 2 == 0 else i + 1)) for g in range(parts) for i in range(1, size - 1)]
    across += [(g * size + i, (g + 1) % parts * size + i) for g in range(parts) for i in (0, size - 1)]
    schur = schur.reshape(3 * face, 3 * face)
    block = ((face, loads), f32)
    field = ((n_rows, loads), f32)
    factor = ((n_rows, tiles * top), bf16)
    steps = tiles // tiles_at_once(tiles, top)

    arrays = (
        iterate,
        v_basis,
        send_rows.reshape(3, 1, face),
        send_count.reshape(3),
        tile_rank.reshape(tiles),
        schur,
        u_basis.reshape(tiles * top, n_rows),
        near_block,
        rhs,
        precond.reshape(1, n_rows),
    )
    square = lambda a: (a.shape, a.dtype)
    coeff, out_a, out_m, out_b, sel, x, schur, u, near, rhs, p = call(
        send_kernel,
        "send",
        [((tiles, top, loads), f32), block, block, block, ((n_rows, 3 * face), bf16), field]
        + [square(arrays[i]) for i in (5, 6, 7, 8, 9)],
        [pltpu.with_memory_space_constraint(a, pltpu.HBM) for a in arrays],
        [HBM] * len(arrays),
        [HBM] + [VMEM] * 10,
        [
            pltpu.VMEM((tiles, top, n_rows), f32),
            pltpu.VMEM((3, 1, face), jnp.int32),
            pltpu.SMEM((3,), jnp.int32),
            pltpu.SMEM((tiles,), jnp.int32),
            pltpu.VMEM((tiles, top, loads), f32),
            pltpu.SemaphoreType.DMA((len(arrays) + 2,)),
            pltpu.SemaphoreType.DMA((steps,)),
        ],
        [pltpu.HBM] + [pltpu.VMEM] * 10,
    )
    order = [(i + lead(size)) % size for i in range(size)]
    gathered = lax.all_to_all(coeff, "wide", split_axis=0, concat_axis=0, tiled=True, axis_index_groups=[order])
    in_a = lax.ppermute(out_a, "wide", inside)
    got = lax.ppermute(out_b, ("groups", "wide"), across)
    pay, part = call(
        across_kernel, "across", [((2 * face, loads), f32)] * 2, (in_a, out_m, schur)
    )
    sums = lax.ppermute(pay, ("groups", "wide"), across)
    base, u_hi, u_lo, scale = call(
        base_kernel, "base", [field, factor, factor, field], (rhs, near, x, u, p, part)
    )
    (f_a,) = call(force_kernel, "force", [block], (got, part, schur))
    back = lax.ppermute(f_a, "wide", inside)
    (base,) = call(own_kernel, "own", [field], (got, part, schur, sel, base))
    (base,) = call(back_kernel, "back", [field], (sums, out_b, back, sel, base))
    return call(
        final_kernel,
        "final",
        [field, field],
        (gathered.reshape(tiles * top, loads), u_hi, u_lo, base, x, scale),
        spaces=[jax.ShapeDtypeStruct] * 2,
    )


def solution(mesh):
    rows = P(("groups", "wide"), None)
    block = P(("groups", "wide"), None, None)
    basis = P("groups", None, "wide")
    in_specs = (rows, rows, block, rows, basis, basis, P("groups", "wide"), block, rows, P(("groups", "wide")))
    return jax.shard_map(body, mesh=mesh, in_specs=in_specs, out_specs=(rows, rows), check_vma=False)
```

```python
import math

import jax
import jax.numpy as jnp
from jax import lax
from jax.experimental import pallas as pl
from jax.experimental.pallas import tpu as pltpu
from jax.sharding import PartitionSpec as P

VMEM = pl.BlockSpec(memory_space=pltpu.VMEM)
HBM = pl.BlockSpec(memory_space=pltpu.HBM)
f32 = jnp.float32
bf16 = jnp.bfloat16


def halves(a):
    hi = a.astype(bf16)
    return hi, (a - hi.astype(f32)).astype(bf16)


def dot(a, b):
    return jnp.dot(a, b, preferred_element_type=f32)


def wide_halves(a):
    return jnp.concatenate(halves(a), axis=1)


def fold(both):
    n = both.shape[1] // 2
    return both[:, :n] + both[:, n:]


def split_product(hi, lo, b_wide):
    n = b_wide.shape[1] // 2
    both = dot(hi, b_wide)
    return both[:, :n] + (both[:, n:] + dot(lo, b_wide[:, :n]))


def product(a, b_wide):
    return split_product(*halves(a), b_wide)


def is_odd():
    return lax.axis_index("wide") % 2 == 1


def lead(size):
    pairs = size // 2
    return (2 * (pairs // 2 + math.isqrt(pairs) // 2) + 1) % size


def turned(hbm, ref, by):
    rest = hbm.shape[0] - by
    if by == 0:
        return [(hbm, ref)]
    return [(hbm.at[pl.ds(by, rest)], ref.at[pl.ds(0, rest)]), (hbm.at[pl.ds(0, by)], ref.at[pl.ds(rest, by)])]


def tiles_at_once(tiles, top):
    return math.gcd(tiles, max(1, 256 // top))


def send_kernel(x_hbm, v_hbm, rows_hbm, count_hbm, rank_hbm, schur_hbm, u_hbm, near_hbm, rhs_hbm, p_hbm,
                coeff_hbm, a_ref, m_ref, b_ref, sel_ref, x_ref, schur_ref, u_ref, near_ref, rhs_ref, p_ref,
                v_ref, rows_ref, count_ref, rank_ref, coeff_ref, sems, out_sems):
    n_rows, loads = x_ref.shape
    face = rows_ref.shape[2]
    tiles, top, _ = v_ref.shape
    first = lead(tiles)
    early = [(x_hbm, x_ref), (rank_hbm, rank_ref)] + turned(v_hbm, v_ref, first)
    middle = [(rows_hbm, rows_ref), (count_hbm, count_ref)]
    late = [(schur_hbm, schur_ref)] + turned(u_hbm, u_ref, first * top)
    late += [(near_hbm, near_ref), (rhs_hbm, rhs_ref), (p_hbm, p_ref)]
    moves = [pltpu.make_async_copy(src, dst, sems.at[i]) for i, (src, dst) in enumerate(early + middle + late)]
    for move in moves:
        move.start()
    moves[0].wait()
    x_wide = wide_halves(x_ref[...])
    for move in moves[1 : len(early)]:
        move.wait()
    step = tiles_at_once(tiles, top)
    k = lax.broadcasted_iota(jnp.int32, (top, loads), 0)

    def out_move(s):
        span = pl.ds(s * step, step)
        return pltpu.make_async_copy(coeff_ref.at[span], coeff_hbm.at[span], out_sems.at[s])

    for s in range(tiles // step):
        part = v_ref[s * step : (s + 1) * step].reshape(step * top, n_rows)
        out = product(part, x_wide).reshape(step, top, loads)
        for t in range(step):
            at = s * step + t
            coeff_ref[at] = jnp.where(k < rank_ref[(at + first) % tiles], out[t], 0.0)
        out_move(s).start()
    for move in moves[len(early) : -len(late)]:
        move.wait()
    odd = is_odd()
    slots = (jnp.where(odd, 0, 2), 1, jnp.where(odd, 2, 0))
    lane = lax.broadcasted_iota(jnp.int32, (1, face), 1)
    across = lax.broadcasted_iota(jnp.int32, (face, n_rows), 1).astype(f32)
    down = lax.broadcasted_iota(jnp.int32, (n_rows, face), 0)
    for spot, out_ref in enumerate((a_ref, m_ref, b_ref)):
        rows = jnp.where(lane < count_ref[slots[spot]], rows_ref[slots[spot]], -1)
        sel_ref[:, spot * face : (spot + 1) * face] = (down == rows).astype(f32).astype(bf16)
        column = jnp.broadcast_to(rows.astype(f32), (face, face)).T[:, :1]
        select = (across == column).astype(f32).astype(bf16)
        out_ref[...] = fold(dot(select, x_wide))
    for s in range(tiles // step):
        out_move(s).wait()
    for move in moves[-len(late) :]:
        move.wait()


def place(odd, spot, face):
    if spot == 1:
        return face
    return pl.multiple_of(jnp.where(odd == (spot == 0), 2 * face, 0), face)


def across_kernel(a_ref, m_ref, schur_ref, pay_ref, part_ref):
    odd = is_odd()
    face = a_ref.shape[0]
    last = pl.ds(place(odd, 2, face), face)
    known = jnp.concatenate([wide_halves(a_ref[...]), wide_halves(m_ref[...])], axis=0)
    pay_ref[face:] = schur_ref[last, last]
    for spot in (2, 0, 1):
        rows = pl.ds(place(odd, spot, face), face)
        block = jnp.concatenate(
            [schur_ref[rows, pl.ds(place(odd, 0, face), face)], schur_ref[rows, face : 2 * face]], axis=1
        )
        out = product(block, known)
        if spot == 2:
            pay_ref[:face] = out
        else:
            part_ref[spot * face : (spot + 1) * face] = out


def base_kernel(rhs_ref, near_ref, x_ref, u_ref, p_ref, _, base_ref, hi_ref, lo_ref, scale_ref):
    n_rows, loads = x_ref.shape
    base_ref[...] = rhs_ref[...] - product(near_ref[...], wide_halves(x_ref[...]))
    hi_ref[...], lo_ref[...] = halves(u_ref[...].T)
    scale_ref[...] = jnp.broadcast_to(p_ref[...], (loads, n_rows)).T


def force_kernel(got_ref, part_ref, schur_ref, fa_ref):
    odd = is_odd()
    face = fa_ref.shape[0]
    block = schur_ref[pl.ds(place(odd, 0, face), face), pl.ds(place(odd, 2, face), face)]
    fa_ref[...] = part_ref[:face] + product(block, wide_halves(got_ref[...]))


def own_kernel(got_ref, part_ref, schur_ref, sel_ref, base_ref, next_ref):
    odd = is_odd()
    face = got_ref.shape[0]
    block = schur_ref[face : 2 * face, pl.ds(place(odd, 2, face), face)]
    own = part_ref[face:] + product(block, wide_halves(got_ref[...]))
    next_ref[...] = base_ref[...] - fold(dot(sel_ref[:, face : 2 * face], wide_halves(own)))


def far_kernel(coeff_ref, hi_ref, lo_ref, base_ref, next_ref):
    next_ref[...] = base_ref[...] - split_product(hi_ref[...], lo_ref[...], wide_halves(coeff_ref[...]))


def final_kernel(pay_ref, out_b_ref, back_ref, sel_ref, base_ref, x_ref, scale_ref, up_ref, res_ref):
    face = back_ref.shape[0]
    a = dot(sel_ref[:, :face], wide_halves(back_ref[...]))
    b = pay_ref[:face] + product(pay_ref[face:], wide_halves(out_b_ref[...]))
    b = dot(sel_ref[:, 2 * face :], wide_halves(b))
    res = base_ref[...] - fold(a + b)
    res_ref[...] = res
    up_ref[...] = x_ref[...] + scale_ref[...] * res


def call(kernel, name, outs, operands, in_specs=None, out_specs=None, scratch=(), spaces=None):
    return pl.pallas_call(
        kernel,
        out_shape=tuple(
            space(s, t) for space, (s, t) in zip(spaces or [pltpu.VMEM] * len(outs), outs)
        ),
        in_specs=in_specs or [VMEM] * len(operands),
        out_specs=tuple(out_specs or [VMEM] * len(outs)),
        scratch_shapes=list(scratch),
        compiler_params=pltpu.CompilerParams(vmem_limit_bytes=40 * 2**20),
        name=name,
    )(*operands)


def body(iterate, rhs, schur, near_block, u_basis, v_basis, tile_rank, send_rows, send_count, precond):
    n_rows, loads = iterate.shape
    face = send_rows.shape[2]
    tiles, top, _ = u_basis.shape
    size = lax.axis_size("wide")
    parts = lax.axis_size("groups")
    inside = [(i, i ^ 1) for i in range(size) if i ^ 1 < size]
    across = [(g * size + i, g * size + (i - 1 if i % 2 == 0 else i + 1)) for g in range(parts) for i in range(1, size - 1)]
    across += [(g * size + i, (g + 1) % parts * size + i) for g in range(parts) for i in (0, size - 1)]
    schur = schur.reshape(3 * face, 3 * face)
    block = ((face, loads), f32)
    field = ((n_rows, loads), f32)
    factor = ((n_rows, tiles * top), bf16)
    steps = tiles // tiles_at_once(tiles, top)

    arrays = (
        iterate,
        v_basis,
        send_rows.reshape(3, 1, face),
        send_count.reshape(3),
        tile_rank.reshape(tiles),
        schur,
        u_basis.reshape(tiles * top, n_rows),
        near_block,
        rhs,
        precond.reshape(1, n_rows),
    )
    square = lambda a: (a.shape, a.dtype)
    coeff, out_a, out_m, out_b, sel, x, schur, u, near, rhs, p = call(
        send_kernel,
        "send",
        [((tiles, top, loads), f32), block, block, block, ((n_rows, 3 * face), bf16), field]
        + [square(arrays[i]) for i in (5, 6, 7, 8, 9)],
        [pltpu.with_memory_space_constraint(a, pltpu.HBM) for a in arrays],
        [HBM] * len(arrays),
        [HBM] + [VMEM] * 10,
        [
            pltpu.VMEM((tiles, top, n_rows), f32),
            pltpu.VMEM((3, 1, face), jnp.int32),
            pltpu.SMEM((3,), jnp.int32),
            pltpu.SMEM((tiles,), jnp.int32),
            pltpu.VMEM((tiles, top, loads), f32),
            pltpu.SemaphoreType.DMA((len(arrays) + 2,)),
            pltpu.SemaphoreType.DMA((steps,)),
        ],
        [pltpu.HBM] + [pltpu.VMEM] * 10,
    )
    order = [(i + lead(size)) % size for i in range(size)]
    gathered = lax.all_to_all(coeff, "wide", split_axis=0, concat_axis=0, tiled=True, axis_index_groups=[order])
    in_a = lax.ppermute(out_a, "wide", inside)
    got = lax.ppermute(out_b, ("groups", "wide"), across)
    pay, part = call(
        across_kernel, "across", [((2 * face, loads), f32)] * 2, (in_a, out_m, schur)
    )
    sums = lax.ppermute(pay, ("groups", "wide"), across)
    base, u_hi, u_lo, scale = call(
        base_kernel, "base", [field, factor, factor, field], (rhs, near, x, u, p, part)
    )
    (f_a,) = call(force_kernel, "force", [block], (got, part, schur))
    back = lax.ppermute(f_a, "wide", inside)
    (base,) = call(own_kernel, "own", [field], (got, part, schur, sel, base))
    (base,) = call(far_kernel, "far", [field], (gathered.reshape(tiles * top, loads), u_hi, u_lo, base))
    return call(
        final_kernel,
        "final",
        [field, field],
        (sums, out_b, back, sel, base, x, scale),
        spaces=[jax.ShapeDtypeStruct] * 2,
    )


def solution(mesh):
    rows = P(("groups", "wide"), None)
    block = P(("groups", "wide"), None, None)
    basis = P("groups", None, "wide")
    in_specs = (rows, rows, block, rows, basis, basis, P("groups", "wide"), block, rows, P(("groups", "wide")))
    return jax.shard_map(body, mesh=mesh, in_specs=in_specs, out_specs=(rows, rows), check_vma=False)
```

```python
import math

import jax
import jax.numpy as jnp
from jax import lax
from jax.experimental import pallas as pl
from jax.experimental.pallas import tpu as pltpu
from jax.sharding import PartitionSpec as P

VMEM = pl.BlockSpec(memory_space=pltpu.VMEM)
HBM = pl.BlockSpec(memory_space=pltpu.HBM)
f32 = jnp.float32
bf16 = jnp.bfloat16


def halves(a):
    hi = a.astype(bf16)
    return hi, (a - hi.astype(f32)).astype(bf16)


def dot(a, b):
    return jnp.dot(a, b, preferred_element_type=f32)


def wide_halves(a):
    return jnp.concatenate(halves(a), axis=1)


def fold(both):
    n = both.shape[1] // 2
    return both[:, :n] + both[:, n:]


def split_product(hi, lo, b_wide):
    n = b_wide.shape[1] // 2
    both = dot(hi, b_wide)
    return both[:, :n] + (both[:, n:] + dot(lo, b_wide[:, :n]))


def product(a, b_wide):
    return split_product(*halves(a), b_wide)


def is_odd():
    return lax.axis_index("wide") % 2 == 1


def group_order(size):
    pairs = size // 2
    first = 2 * (pairs // 2 + math.isqrt(pairs) // 2) + 1
    stride = 5 if math.gcd(5, size) == 1 else 1
    return [(first + stride * i) % size for i in range(size)]


def tiles_at_once(tiles, top):
    return math.gcd(tiles, max(1, 256 // top))


def send_kernel(x_hbm, v_hbm, rows_hbm, count_hbm, rank_hbm, schur_hbm, u_hbm, near_hbm, rhs_hbm, p_hbm,
                coeff_hbm, a_ref, m_ref, b_ref, sel_ref, x_ref, schur_ref, u_ref, near_ref, rhs_ref, p_ref,
                v_ref, rows_ref, count_ref, rank_ref, coeff_ref, sems, out_sems):
    n_rows, loads = x_ref.shape
    face = rows_ref.shape[2]
    tiles, top, _ = v_ref.shape
    order = group_order(tiles)
    early = [(x_hbm, x_ref), (rank_hbm, rank_ref), (v_hbm, v_ref)]
    middle = [(rows_hbm, rows_ref), (count_hbm, count_ref)]
    late = [(schur_hbm, schur_ref), (u_hbm, u_ref), (near_hbm, near_ref), (rhs_hbm, rhs_ref), (p_hbm, p_ref)]
    moves = [pltpu.make_async_copy(src, dst, sems.at[i]) for i, (src, dst) in enumerate(early + middle + late)]
    for move in moves:
        move.start()
    moves[0].wait()
    x_wide = wide_halves(x_ref[...])
    for move in moves[1 : len(early)]:
        move.wait()
    step = tiles_at_once(tiles, top)
    k = lax.broadcasted_iota(jnp.int32, (top, loads), 0)

    def out_move(s):
        span = pl.ds(s * step, step)
        return pltpu.make_async_copy(coeff_ref.at[span], coeff_hbm.at[span], out_sems.at[s])

    for s in range(tiles // step):
        chosen = order[s * step : (s + 1) * step]
        part = jnp.concatenate([v_ref[tile] for tile in chosen], axis=0)
        out = product(part, x_wide).reshape(step, top, loads)
        for t, tile in enumerate(chosen):
            coeff_ref[s * step + t] = jnp.where(k < rank_ref[tile], out[t], 0.0)
        out_move(s).start()
    for move in moves[len(early) : -len(late)]:
        move.wait()
    odd = is_odd()
    slots = (jnp.where(odd, 0, 2), 1, jnp.where(odd, 2, 0))
    lane = lax.broadcasted_iota(jnp.int32, (1, face), 1)
    across = lax.broadcasted_iota(jnp.int32, (face, n_rows), 1).astype(f32)
    down = lax.broadcasted_iota(jnp.int32, (n_rows, face), 0)
    for spot, out_ref in enumerate((a_ref, m_ref, b_ref)):
        rows = jnp.where(lane < count_ref[slots[spot]], rows_ref[slots[spot]], -1)
        sel_ref[:, spot * face : (spot + 1) * face] = (down == rows).astype(f32).astype(bf16)
        column = jnp.broadcast_to(rows.astype(f32), (face, face)).T[:, :1]
        select = (across == column).astype(f32).astype(bf16)
        out_ref[...] = fold(dot(select, x_wide))
    for s in range(tiles // step):
        out_move(s).wait()
    for move in moves[-len(late) :]:
        move.wait()


def place(odd, spot, face):
    if spot == 1:
        return face
    return pl.multiple_of(jnp.where(odd == (spot == 0), 2 * face, 0), face)


def across_kernel(a_ref, m_ref, schur_ref, pay_ref, part_ref):
    odd = is_odd()
    face = a_ref.shape[0]
    last = pl.ds(place(odd, 2, face), face)
    known = jnp.concatenate([wide_halves(a_ref[...]), wide_halves(m_ref[...])], axis=0)
    pay_ref[face:] = schur_ref[last, last]
    for spot in (2, 0, 1):
        rows = pl.ds(place(odd, spot, face), face)
        block = jnp.concatenate(
            [schur_ref[rows, pl.ds(place(odd, 0, face), face)], schur_ref[rows, face : 2 * face]], axis=1
        )
        out = product(block, known)
        if spot == 2:
            pay_ref[:face] = out
        else:
            part_ref[spot * face : (spot + 1) * face] = out


def base_kernel(rhs_ref, near_ref, x_ref, u_ref, p_ref, _, base_ref, hi_ref, lo_ref, scale_ref):
    n_rows, loads = x_ref.shape
    base_ref[...] = rhs_ref[...] - product(near_ref[...], wide_halves(x_ref[...]))
    tiles, top, _ = u_ref.shape
    u = jnp.concatenate([u_ref[tile] for tile in group_order(tiles)], axis=0)
    hi_ref[...], lo_ref[...] = halves(u.T)
    scale_ref[...] = jnp.broadcast_to(p_ref[...], (loads, n_rows)).T


def force_kernel(got_ref, part_ref, schur_ref, fa_ref):
    odd = is_odd()
    face = fa_ref.shape[0]
    block = schur_ref[pl.ds(place(odd, 0, face), face), pl.ds(place(odd, 2, face), face)]
    fa_ref[...] = part_ref[:face] + product(block, wide_halves(got_ref[...]))


def own_kernel(got_ref, part_ref, schur_ref, sel_ref, base_ref, next_ref):
    odd = is_odd()
    face = got_ref.shape[0]
    block = schur_ref[face : 2 * face, pl.ds(place(odd, 2, face), face)]
    own = part_ref[face:] + product(block, wide_halves(got_ref[...]))
    next_ref[...] = base_ref[...] - fold(dot(sel_ref[:, face : 2 * face], wide_halves(own)))


def far_kernel(coeff_ref, hi_ref, lo_ref, base_ref, next_ref):
    next_ref[...] = base_ref[...] - split_product(hi_ref[...], lo_ref[...], wide_halves(coeff_ref[...]))


def final_kernel(pay_ref, out_b_ref, back_ref, sel_ref, base_ref, x_ref, scale_ref, up_ref, res_ref):
    face = back_ref.shape[0]
    a = dot(sel_ref[:, :face], wide_halves(back_ref[...]))
    b = pay_ref[:face] + product(pay_ref[face:], wide_halves(out_b_ref[...]))
    b = dot(sel_ref[:, 2 * face :], wide_halves(b))
    res = base_ref[...] - fold(a + b)
    res_ref[...] = res
    up_ref[...] = x_ref[...] + scale_ref[...] * res


def call(kernel, name, outs, operands, in_specs=None, out_specs=None, scratch=(), spaces=None):
    return pl.pallas_call(
        kernel,
        out_shape=tuple(
            space(s, t) for space, (s, t) in zip(spaces or [pltpu.VMEM] * len(outs), outs)
        ),
        in_specs=in_specs or [VMEM] * len(operands),
        out_specs=tuple(out_specs or [VMEM] * len(outs)),
        scratch_shapes=list(scratch),
        compiler_params=pltpu.CompilerParams(vmem_limit_bytes=40 * 2**20),
        name=name,
    )(*operands)


def body(iterate, rhs, schur, near_block, u_basis, v_basis, tile_rank, send_rows, send_count, precond):
    n_rows, loads = iterate.shape
    face = send_rows.shape[2]
    tiles, top, _ = u_basis.shape
    size = lax.axis_size("wide")
    parts = lax.axis_size("groups")
    inside = [(i, i ^ 1) for i in range(size) if i ^ 1 < size]
    across = [(g * size + i, g * size + (i - 1 if i % 2 == 0 else i + 1)) for g in range(parts) for i in range(1, size - 1)]
    across += [(g * size + i, (g + 1) % parts * size + i) for g in range(parts) for i in (0, size - 1)]
    schur = schur.reshape(3 * face, 3 * face)
    block = ((face, loads), f32)
    field = ((n_rows, loads), f32)
    factor = ((n_rows, tiles * top), bf16)
    steps = tiles // tiles_at_once(tiles, top)

    arrays = (
        iterate,
        v_basis,
        send_rows.reshape(3, 1, face),
        send_count.reshape(3),
        tile_rank.reshape(tiles),
        schur,
        u_basis,
        near_block,
        rhs,
        precond.reshape(1, n_rows),
    )
    square = lambda a: (a.shape, a.dtype)
    coeff, out_a, out_m, out_b, sel, x, schur, u, near, rhs, p = call(
        send_kernel,
        "send",
        [((tiles, top, loads), f32), block, block, block, ((n_rows, 3 * face), bf16), field]
        + [square(arrays[i]) for i in (5, 6, 7, 8, 9)],
        [pltpu.with_memory_space_constraint(a, pltpu.HBM) for a in arrays],
        [HBM] * len(arrays),
        [HBM] + [VMEM] * 10,
        [
            pltpu.VMEM((tiles, top, n_rows), f32),
            pltpu.VMEM((3, 1, face), jnp.int32),
            pltpu.SMEM((3,), jnp.int32),
            pltpu.SMEM((tiles,), jnp.int32),
            pltpu.VMEM((tiles, top, loads), f32),
            pltpu.SemaphoreType.DMA((len(arrays),)),
            pltpu.SemaphoreType.DMA((steps,)),
        ],
        [pltpu.HBM] + [pltpu.VMEM] * 10,
    )
    gathered = lax.all_to_all(
        coeff, "wide", split_axis=0, concat_axis=0, tiled=True, axis_index_groups=[group_order(size)]
    )
    in_a = lax.ppermute(out_a, "wide", inside)
    got = lax.ppermute(out_b, ("groups", "wide"), across)
    pay, part = call(
        across_kernel, "across", [((2 * face, loads), f32)] * 2, (in_a, out_m, schur)
    )
    sums = lax.ppermute(pay, ("groups", "wide"), across)
    base, u_hi, u_lo, scale = call(
        base_kernel, "base", [field, factor, factor, field], (rhs, near, x, u, p, part)
    )
    (f_a,) = call(force_kernel, "force", [block], (got, part, schur))
    back = lax.ppermute(f_a, "wide", inside)
    (base,) = call(own_kernel, "own", [field], (got, part, schur, sel, base))
    (base,) = call(far_kernel, "far", [field], (gathered.reshape(tiles * top, loads), u_hi, u_lo, base))
    return call(
        final_kernel,
        "final",
        [field, field],
        (sums, out_b, back, sel, base, x, scale),
        spaces=[jax.ShapeDtypeStruct] * 2,
    )


def solution(mesh):
    rows = P(("groups", "wide"), None)
    block = P(("groups", "wide"), None, None)
    basis = P("groups", None, "wide")
    in_specs = (rows, rows, block, rows, basis, basis, P("groups", "wide"), block, rows, P(("groups", "wide")))
    return jax.shard_map(body, mesh=mesh, in_specs=in_specs, out_specs=(rows, rows), check_vma=False)
```

```python
import math

import jax
import jax.numpy as jnp
from jax import lax
from jax.experimental import pallas as pl
from jax.experimental.pallas import tpu as pltpu
from jax.sharding import PartitionSpec as P

VMEM = pl.BlockSpec(memory_space=pltpu.VMEM)
HBM = pl.BlockSpec(memory_space=pltpu.HBM)
f32 = jnp.float32
bf16 = jnp.bfloat16


def halves(a):
    hi = a.astype(bf16)
    return hi, (a - hi.astype(f32)).astype(bf16)


def dot(a, b):
    return jnp.dot(a, b, preferred_element_type=f32)


def wide_halves(a):
    return jnp.concatenate(halves(a), axis=1)


def fold(both):
    n = both.shape[1] // 2
    return both[:, :n] + both[:, n:]


def split_product(hi, lo, b_wide):
    n = b_wide.shape[1] // 2
    both = dot(hi, b_wide)
    return both[:, :n] + (both[:, n:] + dot(lo, b_wide[:, :n]))


def product(a, b_wide):
    return split_product(*halves(a), b_wide)


def is_odd():
    return lax.axis_index("wide") % 2 == 1


def group_order(size):
    pairs = size // 2
    first = 2 * (pairs // 2 + math.isqrt(pairs) // 2) + 1
    stride = 5 if math.gcd(5, size) == 1 else 1
    return [(first + stride * i) % size for i in range(size)]


def tiles_at_once(tiles, top):
    return math.gcd(tiles, max(1, 256 // top))


def send_kernel(x_hbm, v_hbm, rows_hbm, count_hbm, rank_hbm, schur_hbm, u_hbm, near_hbm, rhs_hbm, p_hbm,
                coeff_hbm, a_ref, m_ref, b_ref, corner_ref, sel_ref, x_ref, schur_ref, u_ref, near_ref, rhs_ref, p_ref,
                v_ref, rows_ref, count_ref, rank_ref, coeff_ref, sems, out_sems):
    n_rows, loads = x_ref.shape
    face = rows_ref.shape[2]
    tiles, top, _ = v_ref.shape
    order = group_order(tiles)
    early = [(x_hbm, x_ref), (rank_hbm, rank_ref), (v_hbm, v_ref)]
    middle = [(rows_hbm, rows_ref), (count_hbm, count_ref)]
    late = [(schur_hbm, schur_ref), (u_hbm, u_ref), (near_hbm, near_ref), (rhs_hbm, rhs_ref), (p_hbm, p_ref)]
    moves = [pltpu.make_async_copy(src, dst, sems.at[i]) for i, (src, dst) in enumerate(early + middle + late)]
    for move in moves:
        move.start()
    moves[0].wait()
    x_wide = wide_halves(x_ref[...])
    for move in moves[1 : len(early)]:
        move.wait()
    step = tiles_at_once(tiles, top)
    k = lax.broadcasted_iota(jnp.int32, (top, loads), 0)

    def out_move(s):
        span = pl.ds(s * step, step)
        return pltpu.make_async_copy(coeff_ref.at[span], coeff_hbm.at[span], out_sems.at[s])

    for s in range(tiles // step):
        chosen = order[s * step : (s + 1) * step]
        part = jnp.concatenate([v_ref[tile] for tile in chosen], axis=0)
        out = product(part, x_wide).reshape(step, top, loads)
        for t, tile in enumerate(chosen):
            coeff_ref[s * step + t] = jnp.where(k < rank_ref[tile], out[t], 0.0)
        out_move(s).start()
    for move in moves[len(early) : -len(late)]:
        move.wait()
    odd = is_odd()
    slots = (jnp.where(odd, 0, 2), 1, jnp.where(odd, 2, 0))
    lane = lax.broadcasted_iota(jnp.int32, (1, face), 1)
    across = lax.broadcasted_iota(jnp.int32, (face, n_rows), 1).astype(f32)
    down = lax.broadcasted_iota(jnp.int32, (n_rows, face), 0)
    for spot, out_ref in enumerate((a_ref, m_ref, b_ref)):
        rows = jnp.where(lane < count_ref[slots[spot]], rows_ref[slots[spot]], -1)
        sel_ref[:, spot * face : (spot + 1) * face] = (down == rows).astype(f32).astype(bf16)
        column = jnp.broadcast_to(rows.astype(f32), (face, face)).T[:, :1]
        select = (across == column).astype(f32).astype(bf16)
        out_ref[...] = fold(dot(select, x_wide))
    for s in range(tiles // step):
        out_move(s).wait()
    for move in moves[-len(late) :]:
        move.wait()
    last = pl.ds(place(odd, 2, face), face)
    corner_ref[...] = schur_ref[last, last]


def place(odd, spot, face):
    if spot == 1:
        return face
    return pl.multiple_of(jnp.where(odd == (spot == 0), 2 * face, 0), face)


def across_kernel(a_ref, m_ref, schur_ref, pay_ref, part_ref):
    odd = is_odd()
    face = a_ref.shape[0]
    known = jnp.concatenate([wide_halves(a_ref[...]), wide_halves(m_ref[...])], axis=0)
    for spot in (2, 0, 1):
        rows = pl.ds(place(odd, spot, face), face)
        block = jnp.concatenate(
            [schur_ref[rows, pl.ds(place(odd, 0, face), face)], schur_ref[rows, face : 2 * face]], axis=1
        )
        out = product(block, known)
        if spot == 2:
            pay_ref[...] = out
        else:
            part_ref[spot * face : (spot + 1) * face] = out


def base_kernel(rhs_ref, near_ref, x_ref, u_ref, p_ref, _, base_ref, hi_ref, lo_ref, scale_ref):
    n_rows, loads = x_ref.shape
    base_ref[...] = rhs_ref[...] - product(near_ref[...], wide_halves(x_ref[...]))
    tiles, top, _ = u_ref.shape
    u = jnp.concatenate([u_ref[tile] for tile in group_order(tiles)], axis=0)
    hi_ref[...], lo_ref[...] = halves(u.T)
    scale_ref[...] = jnp.broadcast_to(p_ref[...], (loads, n_rows)).T


def force_kernel(got_ref, part_ref, schur_ref, fa_ref):
    odd = is_odd()
    face = fa_ref.shape[0]
    block = schur_ref[pl.ds(place(odd, 0, face), face), pl.ds(place(odd, 2, face), face)]
    fa_ref[...] = part_ref[:face] + product(block, wide_halves(got_ref[...]))


def own_kernel(got_ref, corner_ref, out_b_ref, part_ref, schur_ref, sel_ref, base_ref, next_ref):
    odd = is_odd()
    face = got_ref.shape[0]
    block = schur_ref[face : 2 * face, pl.ds(place(odd, 2, face), face)]
    own = part_ref[face:] + product(block, wide_halves(got_ref[...]))
    back = product(corner_ref[...], wide_halves(out_b_ref[...]))
    both = jnp.concatenate([wide_halves(own), wide_halves(back)], axis=0)
    next_ref[...] = base_ref[...] - fold(dot(sel_ref[:, face:], both))


def far_kernel(coeff_ref, hi_ref, lo_ref, base_ref, next_ref):
    next_ref[...] = base_ref[...] - split_product(hi_ref[...], lo_ref[...], wide_halves(coeff_ref[...]))


def final_kernel(sum_ref, back_ref, sel_ref, base_ref, x_ref, scale_ref, up_ref, res_ref):
    face = back_ref.shape[0]
    a = dot(sel_ref[:, :face], wide_halves(back_ref[...]))
    b = dot(sel_ref[:, 2 * face :], wide_halves(sum_ref[...]))
    res = base_ref[...] - fold(a + b)
    res_ref[...] = res
    up_ref[...] = x_ref[...] + scale_ref[...] * res


def call(kernel, name, outs, operands, in_specs=None, out_specs=None, scratch=(), spaces=None):
    return pl.pallas_call(
        kernel,
        out_shape=tuple(
            space(s, t) for space, (s, t) in zip(spaces or [pltpu.VMEM] * len(outs), outs)
        ),
        in_specs=in_specs or [VMEM] * len(operands),
        out_specs=tuple(out_specs or [VMEM] * len(outs)),
        scratch_shapes=list(scratch),
        compiler_params=pltpu.CompilerParams(vmem_limit_bytes=40 * 2**20),
        name=name,
    )(*operands)


def body(iterate, rhs, schur, near_block, u_basis, v_basis, tile_rank, send_rows, send_count, precond):
    n_rows, loads = iterate.shape
    face = send_rows.shape[2]
    tiles, top, _ = u_basis.shape
    size = lax.axis_size("wide")
    parts = lax.axis_size("groups")
    inside = [(i, i ^ 1) for i in range(size) if i ^ 1 < size]
    across = [(g * size + i, g * size + (i - 1 if i % 2 == 0 else i + 1)) for g in range(parts) for i in range(1, size - 1)]
    across += [(g * size + i, (g + 1) % parts * size + i) for g in range(parts) for i in (0, size - 1)]
    schur = schur.reshape(3 * face, 3 * face)
    block = ((face, loads), f32)
    field = ((n_rows, loads), f32)
    factor = ((n_rows, tiles * top), bf16)
    steps = tiles // tiles_at_once(tiles, top)

    arrays = (
        iterate,
        v_basis,
        send_rows.reshape(3, 1, face),
        send_count.reshape(3),
        tile_rank.reshape(tiles),
        schur,
        u_basis,
        near_block,
        rhs,
        precond.reshape(1, n_rows),
    )
    square = lambda a: (a.shape, a.dtype)
    coeff, out_a, out_m, out_b, corner, sel, x, schur, u, near, rhs, p = call(
        send_kernel,
        "send",
        [((tiles, top, loads), f32), block, block, block, ((face, face), f32), ((n_rows, 3 * face), bf16), field]
        + [square(arrays[i]) for i in (5, 6, 7, 8, 9)],
        [pltpu.with_memory_space_constraint(a, pltpu.HBM) for a in arrays],
        [HBM] * len(arrays),
        [HBM] + [VMEM] * 11,
        [
            pltpu.VMEM((tiles, top, n_rows), f32),
            pltpu.VMEM((3, 1, face), jnp.int32),
            pltpu.SMEM((3,), jnp.int32),
            pltpu.SMEM((tiles,), jnp.int32),
            pltpu.VMEM((tiles, top, loads), f32),
            pltpu.SemaphoreType.DMA((len(arrays),)),
            pltpu.SemaphoreType.DMA((steps,)),
        ],
        [pltpu.HBM] + [pltpu.VMEM] * 11,
    )
    gathered = lax.all_to_all(
        coeff, "wide", split_axis=0, concat_axis=0, tiled=True, axis_index_groups=[group_order(size)]
    )
    in_a = lax.ppermute(out_a, "wide", inside)
    got = lax.ppermute(out_b, ("groups", "wide"), across)
    corner = lax.ppermute(corner, ("groups", "wide"), across)
    pay, part = call(across_kernel, "across", [block, ((2 * face, loads), f32)], (in_a, out_m, schur))
    sums = lax.ppermute(pay, ("groups", "wide"), across)
    base, u_hi, u_lo, scale = call(
        base_kernel, "base", [field, factor, factor, field], (rhs, near, x, u, p, part)
    )
    (f_a,) = call(force_kernel, "force", [block], (got, part, schur))
    back = lax.ppermute(f_a, "wide", inside)
    (base,) = call(own_kernel, "own", [field], (got, corner, out_b, part, schur, sel, base))
    (base,) = call(far_kernel, "far", [field], (gathered.reshape(tiles * top, loads), u_hi, u_lo, base))
    return call(
        final_kernel,
        "final",
        [field, field],
        (sums, back, sel, base, x, scale),
        spaces=[jax.ShapeDtypeStruct] * 2,
    )


def solution(mesh):
    rows = P(("groups", "wide"), None)
    block = P(("groups", "wide"), None, None)
    basis = P("groups", None, "wide")
    in_specs = (rows, rows, block, rows, basis, basis, P("groups", "wide"), block, rows, P(("groups", "wide")))
    return jax.shard_map(body, mesh=mesh, in_specs=in_specs, out_specs=(rows, rows), check_vma=False)
```

```python
import math

import jax
import jax.numpy as jnp
from jax import lax
from jax.experimental import pallas as pl
from jax.experimental.pallas import tpu as pltpu
from jax.sharding import PartitionSpec as P

VMEM = pl.BlockSpec(memory_space=pltpu.VMEM)
HBM = pl.BlockSpec(memory_space=pltpu.HBM)
f32 = jnp.float32
bf16 = jnp.bfloat16


def halves(a):
    hi = a.astype(bf16)
    return hi, (a - hi.astype(f32)).astype(bf16)


def dot(a, b):
    return jnp.dot(a, b, preferred_element_type=f32)


def wide_halves(a):
    return jnp.concatenate(halves(a), axis=1)


def fold(both):
    n = both.shape[1] // 2
    return both[:, :n] + both[:, n:]


def split_product(hi, lo, b_wide):
    n = b_wide.shape[1] // 2
    both = dot(hi, b_wide)
    return both[:, :n] + (both[:, n:] + dot(lo, b_wide[:, :n]))


def product(a, b_wide):
    return split_product(*halves(a), b_wide)


def is_odd():
    return lax.axis_index("wide") % 2 == 1


def group_order(size):
    pairs = size // 2
    first = 2 * (pairs // 2 + math.isqrt(pairs) // 2) + 1
    stride = 5 if math.gcd(5, size) == 1 else 1
    return [(first + stride * i) % size for i in range(size)]


def tiles_at_once(tiles, top):
    return math.gcd(tiles, max(1, 256 // top))


def send_kernel(x_hbm, v_hbm, rows_hbm, count_hbm, rank_hbm, schur_hbm, u_hbm, near_hbm, rhs_hbm, p_hbm,
                coeff_hbm, a_ref, m_ref, b_ref, corner_ref, sel_ref, x_ref, schur_ref, u_ref, near_ref, rhs_ref, p_ref,
                v_ref, rows_ref, count_ref, rank_ref, coeff_ref, sems, out_sems):
    n_rows, loads = x_ref.shape
    face = rows_ref.shape[2]
    tiles, top, _ = v_ref.shape
    order = group_order(tiles)
    early = [(x_hbm, x_ref), (rank_hbm, rank_ref), (v_hbm, v_ref)]
    middle = [(rows_hbm, rows_ref), (count_hbm, count_ref)]
    late = [(schur_hbm, schur_ref), (u_hbm, u_ref), (near_hbm, near_ref), (rhs_hbm, rhs_ref), (p_hbm, p_ref)]
    moves = [pltpu.make_async_copy(src, dst, sems.at[i]) for i, (src, dst) in enumerate(early + middle + late)]
    for move in moves:
        move.start()
    moves[0].wait()
    x_wide = wide_halves(x_ref[...])
    for move in moves[1 : len(early)]:
        move.wait()
    step = tiles_at_once(tiles, top)
    k = lax.broadcasted_iota(jnp.int32, (top, loads), 0)

    def out_move(s):
        span = pl.ds(s * step, step)
        return pltpu.make_async_copy(coeff_ref.at[span], coeff_hbm.at[span], out_sems.at[s])

    for s in range(tiles // step):
        chosen = order[s * step : (s + 1) * step]
        part = jnp.concatenate([v_ref[tile] for tile in chosen], axis=0)
        out = product(part, x_wide).reshape(step, top, loads)
        for t, tile in enumerate(chosen):
            coeff_ref[s * step + t] = jnp.where(k < rank_ref[tile], out[t], 0.0)
        out_move(s).start()
    for move in moves[len(early) : -len(late)]:
        move.wait()
    odd = is_odd()
    slots = (jnp.where(odd, 0, 2), 1, jnp.where(odd, 2, 0))
    lane = lax.broadcasted_iota(jnp.int32, (1, face), 1)
    across = lax.broadcasted_iota(jnp.int32, (face, n_rows), 1).astype(f32)
    down = lax.broadcasted_iota(jnp.int32, (n_rows, face), 0)
    for spot, out_ref in enumerate((a_ref, m_ref, b_ref)):
        rows = jnp.where(lane < count_ref[slots[spot]], rows_ref[slots[spot]], -1)
        sel_ref[:, spot * face : (spot + 1) * face] = (down == rows).astype(f32).astype(bf16)
        column = jnp.broadcast_to(rows.astype(f32), (face, face)).T[:, :1]
        select = (across == column).astype(f32).astype(bf16)
        out_ref[...] = fold(dot(select, x_wide))
    for s in range(tiles // step):
        out_move(s).wait()
    for move in moves[-len(late) :]:
        move.wait()
    last = pl.ds(place(odd, 2, face), face)
    corner_ref[...] = schur_ref[last, last]


def inside_part(ref):
    index = lax.axis_index("wide")
    at_end = (index == 0) | (index == lax.axis_size("wide") - 1)
    return jnp.where(at_end, 0.0, ref[...])


def place(odd, spot, face):
    if spot == 1:
        return face
    return pl.multiple_of(jnp.where(odd == (spot == 0), 2 * face, 0), face)


def across_kernel(a_ref, m_ref, schur_ref, pay_ref, part_ref):
    odd = is_odd()
    face = a_ref.shape[0]
    known = jnp.concatenate([wide_halves(a_ref[...]), wide_halves(m_ref[...])], axis=0)
    for spot in (2, 0, 1):
        rows = pl.ds(place(odd, spot, face), face)
        block = jnp.concatenate(
            [schur_ref[rows, pl.ds(place(odd, 0, face), face)], schur_ref[rows, face : 2 * face]], axis=1
        )
        out = product(block, known)
        if spot == 2:
            pay_ref[...] = out
        else:
            part_ref[spot * face : (spot + 1) * face] = out


def base_kernel(rhs_ref, near_ref, x_ref, u_ref, p_ref, _, base_ref, hi_ref, lo_ref, scale_ref):
    n_rows, loads = x_ref.shape
    base_ref[...] = rhs_ref[...] - product(near_ref[...], wide_halves(x_ref[...]))
    tiles, top, _ = u_ref.shape
    u = jnp.concatenate([u_ref[tile] for tile in group_order(tiles)], axis=0)
    hi_ref[...], lo_ref[...] = halves(u.T)
    scale_ref[...] = jnp.broadcast_to(p_ref[...], (loads, n_rows)).T


def force_kernel(got_ref, part_ref, schur_ref, fa_ref):
    odd = is_odd()
    face = fa_ref.shape[0]
    block = schur_ref[pl.ds(place(odd, 0, face), face), pl.ds(place(odd, 2, face), face)]
    fa_ref[...] = part_ref[:face] + product(block, wide_halves(inside_part(got_ref)))


def own_kernel(got_ref, corner_ref, out_b_ref, part_ref, schur_ref, sel_ref, base_ref, next_ref):
    odd = is_odd()
    face = got_ref.shape[0]
    block = schur_ref[face : 2 * face, pl.ds(place(odd, 2, face), face)]
    own = part_ref[face:] + product(block, wide_halves(inside_part(got_ref)))
    back = product(inside_part(corner_ref), wide_halves(out_b_ref[...]))
    both = jnp.concatenate([wide_halves(own), wide_halves(back)], axis=0)
    next_ref[...] = base_ref[...] - fold(dot(sel_ref[:, face:], both))


def far_kernel(coeff_ref, hi_ref, lo_ref, base_ref, next_ref):
    next_ref[...] = base_ref[...] - split_product(hi_ref[...], lo_ref[...], wide_halves(coeff_ref[...]))


def final_kernel(sum_ref, back_ref, sel_ref, base_ref, x_ref, scale_ref, up_ref, res_ref):
    face = back_ref.shape[0]
    a = dot(sel_ref[:, :face], wide_halves(back_ref[...]))
    b = dot(sel_ref[:, 2 * face :], wide_halves(inside_part(sum_ref)))
    res = base_ref[...] - fold(a + b)
    res_ref[...] = res
    up_ref[...] = x_ref[...] + scale_ref[...] * res


def call(kernel, name, outs, operands, in_specs=None, out_specs=None, scratch=(), spaces=None):
    return pl.pallas_call(
        kernel,
        out_shape=tuple(
            space(s, t) for space, (s, t) in zip(spaces or [pltpu.VMEM] * len(outs), outs)
        ),
        in_specs=in_specs or [VMEM] * len(operands),
        out_specs=tuple(out_specs or [VMEM] * len(outs)),
        scratch_shapes=list(scratch),
        compiler_params=pltpu.CompilerParams(vmem_limit_bytes=40 * 2**20),
        name=name,
    )(*operands)


def body(iterate, rhs, schur, near_block, u_basis, v_basis, tile_rank, send_rows, send_count, precond):
    n_rows, loads = iterate.shape
    face = send_rows.shape[2]
    tiles, top, _ = u_basis.shape
    size = lax.axis_size("wide")
    parts = lax.axis_size("groups")
    inside = [(i, i ^ 1) for i in range(size) if i ^ 1 < size]
    across = [(g * size + i, g * size + (i - 1 if i % 2 == 0 else i + 1)) for g in range(parts) for i in range(1, size - 1)]
    across += [(g * size + i, (g + 1) % parts * size + i) for g in range(parts) for i in (0, size - 1)]
    schur = schur.reshape(3 * face, 3 * face)
    block = ((face, loads), f32)
    field = ((n_rows, loads), f32)
    factor = ((n_rows, tiles * top), bf16)
    steps = tiles // tiles_at_once(tiles, top)

    arrays = (
        iterate,
        v_basis,
        send_rows.reshape(3, 1, face),
        send_count.reshape(3),
        tile_rank.reshape(tiles),
        schur,
        u_basis,
        near_block,
        rhs,
        precond.reshape(1, n_rows),
    )
    square = lambda a: (a.shape, a.dtype)
    coeff, out_a, out_m, out_b, corner, sel, x, schur, u, near, rhs, p = call(
        send_kernel,
        "send",
        [((tiles, top, loads), f32), block, block, block, ((face, face), f32), ((n_rows, 3 * face), bf16), field]
        + [square(arrays[i]) for i in (5, 6, 7, 8, 9)],
        [pltpu.with_memory_space_constraint(a, pltpu.HBM) for a in arrays],
        [HBM] * len(arrays),
        [HBM] + [VMEM] * 11,
        [
            pltpu.VMEM((tiles, top, n_rows), f32),
            pltpu.VMEM((3, 1, face), jnp.int32),
            pltpu.SMEM((3,), jnp.int32),
            pltpu.SMEM((tiles,), jnp.int32),
            pltpu.VMEM((tiles, top, loads), f32),
            pltpu.SemaphoreType.DMA((len(arrays),)),
            pltpu.SemaphoreType.DMA((steps,)),
        ],
        [pltpu.HBM] + [pltpu.VMEM] * 11,
    )
    gathered = lax.all_to_all(
        coeff, "wide", split_axis=0, concat_axis=0, tiled=True, axis_index_groups=[group_order(size)]
    )
    in_a = lax.ppermute(out_a, "wide", inside)
    got = lax.ppermute(out_b, ("groups", "wide"), across)
    corner = lax.ppermute(corner, ("groups", "wide"), across)
    pay, part = call(across_kernel, "across", [block, ((2 * face, loads), f32)], (in_a, out_m, schur))
    sums = lax.ppermute(pay, ("groups", "wide"), across)
    base, u_hi, u_lo, scale = call(
        base_kernel, "base", [field, factor, factor, field], (rhs, near, x, u, p, part)
    )
    (f_a,) = call(force_kernel, "force", [block], (got, part, schur))
    back = lax.ppermute(f_a, "wide", inside)
    (base,) = call(own_kernel, "own", [field], (got, corner, out_b, part, schur, sel, base))
    (base,) = call(far_kernel, "far", [field], (gathered.reshape(tiles * top, loads), u_hi, u_lo, base))
    return call(
        final_kernel,
        "final",
        [field, field],
        (sums, back, sel, base, x, scale),
        spaces=[jax.ShapeDtypeStruct] * 2,
    )


def solution(mesh):
    rows = P(("groups", "wide"), None)
    block = P(("groups", "wide"), None, None)
    basis = P("groups", None, "wide")
    in_specs = (rows, rows, block, rows, basis, basis, P("groups", "wide"), block, rows, P(("groups", "wide")))
    return jax.shard_map(body, mesh=mesh, in_specs=in_specs, out_specs=(rows, rows), check_vma=False)
```

```python
import math

import jax
import jax.numpy as jnp
from jax import lax
from jax.experimental import pallas as pl
from jax.experimental.pallas import tpu as pltpu
from jax.sharding import PartitionSpec as P

VMEM = pl.BlockSpec(memory_space=pltpu.VMEM)
HBM = pl.BlockSpec(memory_space=pltpu.HBM)
f32 = jnp.float32
bf16 = jnp.bfloat16


def halves(a):
    hi = a.astype(bf16)
    return hi, (a - hi.astype(f32)).astype(bf16)


def dot(a, b):
    return jnp.dot(a, b, preferred_element_type=f32)


def wide_halves(a):
    return jnp.concatenate(halves(a), axis=1)


def fold(both):
    n = both.shape[1] // 2
    return both[:, :n] + both[:, n:]


def split_product(hi, lo, b_wide):
    n = b_wide.shape[1] // 2
    both = dot(hi, b_wide)
    return both[:, :n] + (both[:, n:] + dot(lo, b_wide[:, :n]))


def product(a, b_wide):
    return split_product(*halves(a), b_wide)


def is_odd():
    return lax.axis_index("wide") % 2 == 1


def group_order(size):
    pairs = size // 2
    first = 2 * (pairs // 2 + math.isqrt(pairs) // 2) + 1
    stride = 5 if math.gcd(5, size) == 1 else 1
    return [(first + stride * i) % size for i in range(size)]


def tiles_at_once(tiles, top):
    return math.gcd(tiles, max(1, 256 // top))


def send_kernel(x_hbm, v_hbm, rows_hbm, count_hbm, rank_hbm, schur_hbm, u_hbm, near_hbm, rhs_hbm, p_hbm,
                coeff_hbm, a_ref, m_ref, b_ref, corner_ref, sel_ref, x_ref, schur_ref, u_ref, near_ref, rhs_ref, p_ref,
                v_ref, rows_ref, count_ref, rank_ref, coeff_ref, sems, out_sems):
    n_rows, loads = x_ref.shape
    face = rows_ref.shape[2]
    tiles, top, _ = v_ref.shape
    order = group_order(tiles)
    early = [(x_hbm, x_ref), (rank_hbm, rank_ref), (v_hbm, v_ref)]
    middle = [(rows_hbm, rows_ref), (count_hbm, count_ref)]
    late = [(schur_hbm, schur_ref), (u_hbm, u_ref), (near_hbm, near_ref), (rhs_hbm, rhs_ref), (p_hbm, p_ref)]
    moves = [pltpu.make_async_copy(src, dst, sems.at[i]) for i, (src, dst) in enumerate(early + middle + late)]
    for move in moves:
        move.start()
    moves[0].wait()
    x_wide = wide_halves(x_ref[...])
    for move in moves[1 : len(early)]:
        move.wait()
    step = tiles_at_once(tiles, top)
    k = lax.broadcasted_iota(jnp.int32, (top, loads), 0)

    def out_move(s):
        span = pl.ds(s * step, step)
        return pltpu.make_async_copy(coeff_ref.at[span], coeff_hbm.at[span], out_sems.at[s])

    for s in range(tiles // step):
        chosen = order[s * step : (s + 1) * step]
        part = jnp.concatenate([v_ref[tile] for tile in chosen], axis=0)
        out = product(part, x_wide).reshape(step, top, loads)
        for t, tile in enumerate(chosen):
            coeff_ref[s * step + t] = jnp.where(k < rank_ref[tile], out[t], 0.0)
        out_move(s).start()
    for move in moves[len(early) : -len(late)]:
        move.wait()
    odd = is_odd()
    slots = (jnp.where(odd, 0, 2), 1, jnp.where(odd, 2, 0))
    lane = lax.broadcasted_iota(jnp.int32, (1, face), 1)
    across = lax.broadcasted_iota(jnp.int32, (face, n_rows), 1).astype(f32)
    down = lax.broadcasted_iota(jnp.int32, (n_rows, face), 0)
    for spot, out_ref in enumerate((a_ref, m_ref, b_ref)):
        rows = jnp.where(lane < count_ref[slots[spot]], rows_ref[slots[spot]], -1)
        column = (0, 2, 1)[spot] * face
        sel_ref[:, column : column + face] = (down == rows).astype(f32).astype(bf16)
        wanted = jnp.broadcast_to(rows.astype(f32), (face, face)).T[:, :1]
        select = (across == wanted).astype(f32).astype(bf16)
        out_ref[...] = fold(dot(select, x_wide))
    for s in range(tiles // step):
        out_move(s).wait()
    for move in moves[-len(late) :]:
        move.wait()
    last = pl.ds(place(odd, 2, face), face)
    corner_ref[...] = schur_ref[last, last]


def inside_part(ref):
    index = lax.axis_index("wide")
    at_end = (index == 0) | (index == lax.axis_size("wide") - 1)
    return jnp.where(at_end, 0.0, ref[...])


def place(odd, spot, face):
    if spot == 1:
        return face
    return pl.multiple_of(jnp.where(odd == (spot == 0), 2 * face, 0), face)


def across_kernel(a_ref, m_ref, schur_ref, pay_ref, part_ref):
    odd = is_odd()
    face = a_ref.shape[0]
    known = jnp.concatenate([wide_halves(a_ref[...]), wide_halves(m_ref[...])], axis=0)
    for spot in (2, 0, 1):
        rows = pl.ds(place(odd, spot, face), face)
        block = jnp.concatenate(
            [schur_ref[rows, pl.ds(place(odd, 0, face), face)], schur_ref[rows, face : 2 * face]], axis=1
        )
        out = product(block, known)
        if spot == 2:
            pay_ref[...] = out
        else:
            part_ref[spot * face : (spot + 1) * face] = out


def base_kernel(rhs_ref, near_ref, x_ref, u_ref, p_ref, _, base_ref, hi_ref, lo_ref, scale_ref):
    n_rows, loads = x_ref.shape
    base_ref[...] = rhs_ref[...] - product(near_ref[...], wide_halves(x_ref[...]))
    tiles, top, _ = u_ref.shape
    u = jnp.concatenate([u_ref[tile] for tile in group_order(tiles)], axis=0)
    hi_ref[...], lo_ref[...] = halves(u.T)
    scale_ref[...] = jnp.broadcast_to(p_ref[...], (loads, n_rows)).T


def force_kernel(got_ref, part_ref, schur_ref, fa_ref):
    odd = is_odd()
    face = fa_ref.shape[0]
    block = schur_ref[pl.ds(place(odd, 0, face), face), pl.ds(place(odd, 2, face), face)]
    fa_ref[...] = part_ref[:face] + product(block, wide_halves(inside_part(got_ref)))


def own_kernel(got_ref, corner_ref, out_b_ref, part_ref, schur_ref, sel_ref, base_ref, next_ref):
    odd = is_odd()
    face = got_ref.shape[0]
    block = schur_ref[face : 2 * face, pl.ds(place(odd, 2, face), face)]
    own = part_ref[face:] + product(block, wide_halves(inside_part(got_ref)))
    back = product(inside_part(corner_ref), wide_halves(out_b_ref[...]))
    both = jnp.concatenate([wide_halves(back), wide_halves(own)], axis=0)
    next_ref[...] = base_ref[...] - fold(dot(sel_ref[:, face:], both))


def far_kernel(coeff_ref, hi_ref, lo_ref, base_ref, next_ref):
    next_ref[...] = base_ref[...] - split_product(hi_ref[...], lo_ref[...], wide_halves(coeff_ref[...]))


def final_kernel(sum_ref, back_ref, sel_ref, base_ref, x_ref, scale_ref, up_ref, res_ref):
    face = back_ref.shape[0]
    both = jnp.concatenate([wide_halves(back_ref[...]), wide_halves(inside_part(sum_ref))], axis=0)
    res = base_ref[...] - fold(dot(sel_ref[:, : 2 * face], both))
    res_ref[...] = res
    up_ref[...] = x_ref[...] + scale_ref[...] * res


def call(kernel, name, outs, operands, in_specs=None, out_specs=None, scratch=(), spaces=None):
    return pl.pallas_call(
        kernel,
        out_shape=tuple(
            space(s, t) for space, (s, t) in zip(spaces or [pltpu.VMEM] * len(outs), outs)
        ),
        in_specs=in_specs or [VMEM] * len(operands),
        out_specs=tuple(out_specs or [VMEM] * len(outs)),
        scratch_shapes=list(scratch),
        compiler_params=pltpu.CompilerParams(vmem_limit_bytes=40 * 2**20),
        name=name,
    )(*operands)


def body(iterate, rhs, schur, near_block, u_basis, v_basis, tile_rank, send_rows, send_count, precond):
    n_rows, loads = iterate.shape
    face = send_rows.shape[2]
    tiles, top, _ = u_basis.shape
    size = lax.axis_size("wide")
    parts = lax.axis_size("groups")
    inside = [(i, i ^ 1) for i in range(size) if i ^ 1 < size]
    across = [(g * size + i, g * size + (i - 1 if i % 2 == 0 else i + 1)) for g in range(parts) for i in range(1, size - 1)]
    across += [(g * size + i, (g + 1) % parts * size + i) for g in range(parts) for i in (0, size - 1)]
    schur = schur.reshape(3 * face, 3 * face)
    block = ((face, loads), f32)
    field = ((n_rows, loads), f32)
    factor = ((n_rows, tiles * top), bf16)
    steps = tiles // tiles_at_once(tiles, top)

    arrays = (
        iterate,
        v_basis,
        send_rows.reshape(3, 1, face),
        send_count.reshape(3),
        tile_rank.reshape(tiles),
        schur,
        u_basis,
        near_block,
        rhs,
        precond.reshape(1, n_rows),
    )
    square = lambda a: (a.shape, a.dtype)
    coeff, out_a, out_m, out_b, corner, sel, x, schur, u, near, rhs, p = call(
        send_kernel,
        "send",
        [((tiles, top, loads), f32), block, block, block, ((face, face), f32), ((n_rows, 3 * face), bf16), field]
        + [square(arrays[i]) for i in (5, 6, 7, 8, 9)],
        [pltpu.with_memory_space_constraint(a, pltpu.HBM) for a in arrays],
        [HBM] * len(arrays),
        [HBM] + [VMEM] * 11,
        [
            pltpu.VMEM((tiles, top, n_rows), f32),
            pltpu.VMEM((3, 1, face), jnp.int32),
            pltpu.SMEM((3,), jnp.int32),
            pltpu.SMEM((tiles,), jnp.int32),
            pltpu.VMEM((tiles, top, loads), f32),
            pltpu.SemaphoreType.DMA((len(arrays),)),
            pltpu.SemaphoreType.DMA((steps,)),
        ],
        [pltpu.HBM] + [pltpu.VMEM] * 11,
    )
    gathered = lax.all_to_all(
        coeff, "wide", split_axis=0, concat_axis=0, tiled=True, axis_index_groups=[group_order(size)]
    )
    in_a = lax.ppermute(out_a, "wide", inside)
    got = lax.ppermute(out_b, ("groups", "wide"), across)
    corner = lax.ppermute(corner, ("groups", "wide"), across)
    pay, part = call(across_kernel, "across", [block, ((2 * face, loads), f32)], (in_a, out_m, schur))
    sums = lax.ppermute(pay, ("groups", "wide"), across)
    base, u_hi, u_lo, scale = call(
        base_kernel, "base", [field, factor, factor, field], (rhs, near, x, u, p, part)
    )
    (f_a,) = call(force_kernel, "force", [block], (got, part, schur))
    back = lax.ppermute(f_a, "wide", inside)
    (base,) = call(own_kernel, "own", [field], (got, corner, out_b, part, schur, sel, base))
    (base,) = call(far_kernel, "far", [field], (gathered.reshape(tiles * top, loads), u_hi, u_lo, base))
    return call(
        final_kernel,
        "final",
        [field, field],
        (sums, back, sel, base, x, scale),
        spaces=[jax.ShapeDtypeStruct] * 2,
    )


def solution(mesh):
    rows = P(("groups", "wide"), None)
    block = P(("groups", "wide"), None, None)
    basis = P("groups", None, "wide")
    in_specs = (rows, rows, block, rows, basis, basis, P("groups", "wide"), block, rows, P(("groups", "wide")))
    return jax.shard_map(body, mesh=mesh, in_specs=in_specs, out_specs=(rows, rows), check_vma=False)
```

```python
import math

import jax
import jax.numpy as jnp
import numpy as np
from jax import lax
from jax.experimental import pallas as pl
from jax.experimental.pallas import tpu as pltpu
from jax.sharding import PartitionSpec as P

VMEM = pl.BlockSpec(memory_space=pltpu.VMEM)
HBM = pl.BlockSpec(memory_space=pltpu.HBM)
f32 = jnp.float32
bf16 = jnp.bfloat16


def halves(a):
    hi = a.astype(bf16)
    return hi, (a - hi.astype(f32)).astype(bf16)


def dot(a, b):
    return jnp.dot(a, b, preferred_element_type=f32)


def wide_halves(a):
    return jnp.concatenate(halves(a), axis=1)


def fold(both):
    n = both.shape[1] // 2
    return both[:, :n] + both[:, n:]


def split_product(hi, lo, b_wide):
    n = b_wide.shape[1] // 2
    both = dot(hi, b_wide)
    return both[:, :n] + (both[:, n:] + dot(lo, b_wide[:, :n]))


def product(a, b_wide):
    return split_product(*halves(a), b_wide)


def is_odd():
    return lax.axis_index("wide") % 2 == 1


def group_order(size):
    pairs = size // 2
    first = 2 * (pairs // 2 + math.isqrt(pairs) // 2) + 1
    rest = [i for i in range(size) if i != first]
    return [first] + [rest[i] for i in np.random.RandomState(12).permutation(size - 1).tolist()]


def tiles_at_once(tiles, top):
    return math.gcd(tiles, max(1, 256 // top))


def send_kernel(x_hbm, v_hbm, rows_hbm, count_hbm, rank_hbm, schur_hbm, u_hbm, near_hbm, rhs_hbm, p_hbm,
                coeff_hbm, a_ref, m_ref, b_ref, corner_ref, sel_ref, x_ref, schur_ref, u_ref, near_ref, rhs_ref, p_ref,
                v_ref, rows_ref, count_ref, rank_ref, coeff_ref, sems, out_sems):
    n_rows, loads = x_ref.shape
    face = rows_ref.shape[2]
    tiles, top, _ = v_ref.shape
    order = group_order(tiles)
    early = [(v_hbm, v_ref), (x_hbm, x_ref), (rank_hbm, rank_ref)]
    middle = [(rows_hbm, rows_ref), (count_hbm, count_ref)]
    late = [(schur_hbm, schur_ref), (u_hbm, u_ref), (near_hbm, near_ref), (rhs_hbm, rhs_ref), (p_hbm, p_ref)]
    moves = [pltpu.make_async_copy(src, dst, sems.at[i]) for i, (src, dst) in enumerate(early + middle + late)]
    for move in moves:
        move.start()
    moves[1].wait()
    x_wide = wide_halves(x_ref[...])
    moves[0].wait()
    moves[2].wait()
    step = tiles_at_once(tiles, top)
    k = lax.broadcasted_iota(jnp.int32, (top, loads), 0)

    def out_move(s):
        span = pl.ds(s * step, step)
        return pltpu.make_async_copy(coeff_ref.at[span], coeff_hbm.at[span], out_sems.at[s])

    for s in range(tiles // step):
        chosen = order[s * step : (s + 1) * step]
        part = jnp.concatenate([v_ref[tile] for tile in chosen], axis=0)
        out = product(part, x_wide).reshape(step, top, loads)
        for t, tile in enumerate(chosen):
            coeff_ref[s * step + t] = jnp.where(k < rank_ref[tile], out[t], 0.0)
        out_move(s).start()
    for move in moves[len(early) : -len(late)]:
        move.wait()
    odd = is_odd()
    slots = (jnp.where(odd, 0, 2), 1, jnp.where(odd, 2, 0))
    lane = lax.broadcasted_iota(jnp.int32, (1, face), 1)
    across = lax.broadcasted_iota(jnp.int32, (face, n_rows), 1).astype(f32)
    down = lax.broadcasted_iota(jnp.int32, (n_rows, face), 0)
    for spot, out_ref in enumerate((a_ref, m_ref, b_ref)):
        rows = jnp.where(lane < count_ref[slots[spot]], rows_ref[slots[spot]], -1)
        column = (0, 2, 1)[spot] * face
        sel_ref[:, column : column + face] = (down == rows).astype(f32).astype(bf16)
        wanted = jnp.broadcast_to(rows.astype(f32), (face, face)).T[:, :1]
        select = (across == wanted).astype(f32).astype(bf16)
        out_ref[...] = fold(dot(select, x_wide))
    for s in range(tiles // step):
        out_move(s).wait()
    for move in moves[-len(late) :]:
        move.wait()
    last = pl.ds(place(odd, 2, face), face)
    corner_ref[...] = schur_ref[last, last]


def inside_part(ref):
    index = lax.axis_index("wide")
    at_end = (index == 0) | (index == lax.axis_size("wide") - 1)
    return jnp.where(at_end, 0.0, ref[...])


def place(odd, spot, face):
    if spot == 1:
        return face
    return pl.multiple_of(jnp.where(odd == (spot == 0), 2 * face, 0), face)


def across_kernel(a_ref, m_ref, schur_ref, pay_ref, part_ref):
    odd = is_odd()
    face = a_ref.shape[0]
    known = jnp.concatenate([wide_halves(a_ref[...]), wide_halves(m_ref[...])], axis=0)
    for spot in (2, 0, 1):
        rows = pl.ds(place(odd, spot, face), face)
        block = jnp.concatenate(
            [schur_ref[rows, pl.ds(place(odd, 0, face), face)], schur_ref[rows, face : 2 * face]], axis=1
        )
        out = product(block, known)
        if spot == 2:
            pay_ref[...] = out
        else:
            part_ref[spot * face : (spot + 1) * face] = out


def base_kernel(rhs_ref, near_ref, x_ref, u_ref, p_ref, _, base_ref, hi_ref, lo_ref, scale_ref):
    n_rows, loads = x_ref.shape
    base_ref[...] = rhs_ref[...] - product(near_ref[...], wide_halves(x_ref[...]))
    tiles, top, _ = u_ref.shape
    u = jnp.concatenate([u_ref[tile] for tile in group_order(tiles)], axis=0)
    hi_ref[...], lo_ref[...] = halves(u.T)
    scale_ref[...] = jnp.broadcast_to(p_ref[...], (loads, n_rows)).T


def force_kernel(got_ref, part_ref, schur_ref, fa_ref):
    odd = is_odd()
    face = fa_ref.shape[0]
    block = schur_ref[pl.ds(place(odd, 0, face), face), pl.ds(place(odd, 2, face), face)]
    fa_ref[...] = part_ref[:face] + product(block, wide_halves(inside_part(got_ref)))


def own_kernel(got_ref, corner_ref, out_b_ref, part_ref, schur_ref, sel_ref, base_ref, next_ref):
    odd = is_odd()
    face = got_ref.shape[0]
    block = schur_ref[face : 2 * face, pl.ds(place(odd, 2, face), face)]
    own = part_ref[face:] + product(block, wide_halves(inside_part(got_ref)))
    back = product(inside_part(corner_ref), wide_halves(out_b_ref[...]))
    both = jnp.concatenate([wide_halves(back), wide_halves(own)], axis=0)
    next_ref[...] = base_ref[...] - fold(dot(sel_ref[:, face:], both))


def far_kernel(coeff_ref, hi_ref, lo_ref, base_ref, next_ref):
    next_ref[...] = base_ref[...] - split_product(hi_ref[...], lo_ref[...], wide_halves(coeff_ref[...]))


def final_kernel(sum_ref, back_ref, sel_ref, base_ref, x_ref, scale_ref, up_ref, res_ref):
    face = back_ref.shape[0]
    both = jnp.concatenate([wide_halves(back_ref[...]), wide_halves(inside_part(sum_ref))], axis=0)
    res = base_ref[...] - fold(dot(sel_ref[:, : 2 * face], both))
    res_ref[...] = res
    up_ref[...] = x_ref[...] + scale_ref[...] * res


def call(kernel, name, outs, operands, in_specs=None, out_specs=None, scratch=(), spaces=None):
    return pl.pallas_call(
        kernel,
        out_shape=tuple(
            space(s, t) for space, (s, t) in zip(spaces or [pltpu.VMEM] * len(outs), outs)
        ),
        in_specs=in_specs or [VMEM] * len(operands),
        out_specs=tuple(out_specs or [VMEM] * len(outs)),
        scratch_shapes=list(scratch),
        compiler_params=pltpu.CompilerParams(vmem_limit_bytes=40 * 2**20),
        name=name,
    )(*operands)


def body(iterate, rhs, schur, near_block, u_basis, v_basis, tile_rank, send_rows, send_count, precond):
    n_rows, loads = iterate.shape
    face = send_rows.shape[2]
    tiles, top, _ = u_basis.shape
    size = lax.axis_size("wide")
    parts = lax.axis_size("groups")
    inside = [(i, i ^ 1) for i in range(size) if i ^ 1 < size]
    across = [(g * size + i, g * size + (i - 1 if i % 2 == 0 else i + 1)) for g in range(parts) for i in range(1, size - 1)]
    across += [(g * size + i, (g + 1) % parts * size + i) for g in range(parts) for i in (0, size - 1)]
    schur = schur.reshape(3 * face, 3 * face)
    block = ((face, loads), f32)
    field = ((n_rows, loads), f32)
    factor = ((n_rows, tiles * top), bf16)
    steps = tiles // tiles_at_once(tiles, top)

    arrays = (
        iterate,
        v_basis,
        send_rows.reshape(3, 1, face),
        send_count.reshape(3),
        tile_rank.reshape(tiles),
        schur,
        u_basis,
        near_block,
        rhs,
        precond.reshape(1, n_rows),
    )
    square = lambda a: (a.shape, a.dtype)
    coeff, out_a, out_m, out_b, corner, sel, x, schur, u, near, rhs, p = call(
        send_kernel,
        "send",
        [((tiles, top, loads), f32), block, block, block, ((face, face), f32), ((n_rows, 3 * face), bf16), field]
        + [square(arrays[i]) for i in (5, 6, 7, 8, 9)],
        [pltpu.with_memory_space_constraint(a, pltpu.HBM) for a in arrays],
        [HBM] * len(arrays),
        [HBM] + [VMEM] * 11,
        [
            pltpu.VMEM((tiles, top, n_rows), f32),
            pltpu.VMEM((3, 1, face), jnp.int32),
            pltpu.SMEM((3,), jnp.int32),
            pltpu.SMEM((tiles,), jnp.int32),
            pltpu.VMEM((tiles, top, loads), f32),
            pltpu.SemaphoreType.DMA((len(arrays),)),
            pltpu.SemaphoreType.DMA((steps,)),
        ],
        [pltpu.HBM] + [pltpu.VMEM] * 11,
    )
    gathered = lax.all_to_all(
        coeff, "wide", split_axis=0, concat_axis=0, tiled=True, axis_index_groups=[group_order(size)]
    )
    in_a = lax.ppermute(out_a, "wide", inside)
    got = lax.ppermute(out_b, ("groups", "wide"), across)
    corner = lax.ppermute(corner, ("groups", "wide"), across)
    pay, part = call(across_kernel, "across", [block, ((2 * face, loads), f32)], (in_a, out_m, schur))
    sums = lax.ppermute(pay, ("groups", "wide"), across)
    base, u_hi, u_lo, scale = call(
        base_kernel, "base", [field, factor, factor, field], (rhs, near, x, u, p, part)
    )
    (f_a,) = call(force_kernel, "force", [block], (got, part, schur))
    back = lax.ppermute(f_a, "wide", inside)
    (base,) = call(own_kernel, "own", [field], (got, corner, out_b, part, schur, sel, base))
    (base,) = call(far_kernel, "far", [field], (gathered.reshape(tiles * top, loads), u_hi, u_lo, base))
    return call(
        final_kernel,
        "final",
        [field, field],
        (sums, back, sel, base, x, scale),
        spaces=[jax.ShapeDtypeStruct] * 2,
    )


def solution(mesh):
    rows = P(("groups", "wide"), None)
    block = P(("groups", "wide"), None, None)
    basis = P("groups", None, "wide")
    in_specs = (rows, rows, block, rows, basis, basis, P("groups", "wide"), block, rows, P(("groups", "wide")))
    return jax.shard_map(body, mesh=mesh, in_specs=in_specs, out_specs=(rows, rows), check_vma=False)
```

```python
import math

import jax
import jax.numpy as jnp
import numpy as np
from jax import lax
from jax.experimental import pallas as pl
from jax.experimental.pallas import tpu as pltpu
from jax.sharding import PartitionSpec as P

VMEM = pl.BlockSpec(memory_space=pltpu.VMEM)
HBM = pl.BlockSpec(memory_space=pltpu.HBM)
f32 = jnp.float32
bf16 = jnp.bfloat16


def halves(a):
    hi = a.astype(bf16)
    return hi, (a - hi.astype(f32)).astype(bf16)


def dot(a, b):
    return jnp.dot(a, b, preferred_element_type=f32)


def wide_halves(a):
    return jnp.concatenate(halves(a), axis=1)


def fold(both):
    n = both.shape[1] // 2
    return both[:, :n] + both[:, n:]


def split_product(hi, lo, b_wide):
    n = b_wide.shape[1] // 2
    both = dot(hi, b_wide)
    return both[:, :n] + (both[:, n:] + dot(lo, b_wide[:, :n]))


def product(a, b_wide):
    return split_product(*halves(a), b_wide)


def is_odd():
    return lax.axis_index("wide") % 2 == 1


def group_order(size):
    pairs = size // 2
    first = 2 * (pairs // 2 + math.isqrt(pairs) // 2) + 1
    rest = [i for i in range(size) if i != first]
    return [first] + [rest[i] for i in np.random.RandomState(12).permutation(size - 1).tolist()]


def tiles_at_once(tiles, top):
    return math.gcd(tiles, max(1, 256 // top))


def send_kernel(x_hbm, v_hbm, rows_hbm, count_hbm, rank_hbm, schur_hbm, u_hbm, near_hbm, rhs_hbm, p_hbm,
                coeff_hbm, a_ref, m_ref, b_ref, corner_ref, sel_ref, x_ref, schur_ref, u_ref, near_ref, rhs_ref, p_ref,
                v_ref, rows_ref, count_ref, rank_ref, coeff_ref, sems, out_sems):
    n_rows, loads = x_ref.shape
    face = rows_ref.shape[2]
    tiles, top, _ = v_ref.shape
    order = group_order(tiles)
    early = [(v_hbm, v_ref), (x_hbm, x_ref), (rank_hbm, rank_ref)]
    middle = [(rows_hbm, rows_ref), (count_hbm, count_ref)]
    late = [(schur_hbm, schur_ref), (u_hbm, u_ref), (near_hbm, near_ref), (rhs_hbm, rhs_ref), (p_hbm, p_ref)]
    moves = [pltpu.make_async_copy(src, dst, sems.at[i]) for i, (src, dst) in enumerate(early + middle + late)]
    for move in moves:
        move.start()
    moves[1].wait()
    x_wide = wide_halves(x_ref[...])
    moves[0].wait()
    moves[2].wait()
    step = tiles_at_once(tiles, top)
    k = lax.broadcasted_iota(jnp.int32, (top, loads), 0)

    def out_move(s):
        span = pl.ds(s * step, step)
        return pltpu.make_async_copy(coeff_ref.at[span], coeff_hbm.at[span], out_sems.at[s])

    for s in range(tiles // step):
        chosen = order[s * step : (s + 1) * step]
        part = jnp.concatenate([v_ref[tile] for tile in chosen], axis=0)
        out = product(part, x_wide).reshape(step, top, loads)
        for t, tile in enumerate(chosen):
            coeff_ref[s * step + t] = jnp.where(k < rank_ref[tile], out[t], 0.0)
        out_move(s).start()
    for move in moves[len(early) : -len(late)]:
        move.wait()
    odd = is_odd()
    slots = (jnp.where(odd, 0, 2), 1, jnp.where(odd, 2, 0))
    lane = lax.broadcasted_iota(jnp.int32, (1, face), 1)
    across = lax.broadcasted_iota(jnp.int32, (face, n_rows), 1).astype(f32)
    down = lax.broadcasted_iota(jnp.int32, (n_rows, face), 0)
    for spot, out_ref in enumerate((a_ref, m_ref, b_ref)):
        rows = jnp.where(lane < count_ref[slots[spot]], rows_ref[slots[spot]], -1)
        column = (0, 2, 1)[spot] * face
        sel_ref[:, column : column + face] = (down == rows).astype(f32).astype(bf16)
        wanted = jnp.broadcast_to(rows.astype(f32), (face, face)).T[:, :1]
        select = (across == wanted).astype(f32).astype(bf16)
        out_ref[...] = fold(dot(select, x_wide))
    for s in range(tiles // step):
        out_move(s).wait()
    for move in moves[-len(late) :]:
        move.wait()
    last = pl.ds(place(odd, 2, face), face)
    corner_ref[...] = schur_ref[last, last]


def inside_part(ref):
    index = lax.axis_index("wide")
    at_end = (index == 0) | (index == lax.axis_size("wide") - 1)
    return jnp.where(at_end, 0.0, ref[...])


def place(odd, spot, face):
    if spot == 1:
        return face
    return pl.multiple_of(jnp.where(odd == (spot == 0), 2 * face, 0), face)


def across_kernel(a_ref, m_ref, schur_ref, pay_ref, part_ref):
    odd = is_odd()
    face = a_ref.shape[0]
    known = jnp.concatenate([wide_halves(a_ref[...]), wide_halves(m_ref[...])], axis=0)
    for spot in (2, 0, 1):
        rows = pl.ds(place(odd, spot, face), face)
        block = jnp.concatenate(
            [schur_ref[rows, pl.ds(place(odd, 0, face), face)], schur_ref[rows, face : 2 * face]], axis=1
        )
        out = product(block, known)
        if spot == 2:
            pay_ref[...] = out
        else:
            part_ref[spot * face : (spot + 1) * face] = out


def base_kernel(rhs_ref, near_ref, x_ref, u_ref, p_ref, _, base_ref, hi_ref, lo_ref, scale_ref):
    n_rows, loads = x_ref.shape
    base_ref[...] = rhs_ref[...] - product(near_ref[...], wide_halves(x_ref[...]))
    tiles, top, _ = u_ref.shape
    u = jnp.concatenate([u_ref[tile] for tile in group_order(tiles)], axis=0)
    hi_ref[...], lo_ref[...] = halves(u.T)
    scale_ref[...] = jnp.broadcast_to(p_ref[...], (loads, n_rows)).T


def force_kernel(got_ref, part_ref, schur_ref, _, fa_ref):
    odd = is_odd()
    face = fa_ref.shape[0]
    block = schur_ref[pl.ds(place(odd, 0, face), face), pl.ds(place(odd, 2, face), face)]
    fa_ref[...] = part_ref[:face] + product(block, wide_halves(inside_part(got_ref)))


def own_kernel(got_ref, corner_ref, out_b_ref, part_ref, schur_ref, sel_ref, base_ref, next_ref):
    odd = is_odd()
    face = got_ref.shape[0]
    block = schur_ref[face : 2 * face, pl.ds(place(odd, 2, face), face)]
    own = part_ref[face:] + product(block, wide_halves(inside_part(got_ref)))
    back = product(inside_part(corner_ref), wide_halves(out_b_ref[...]))
    both = jnp.concatenate([wide_halves(back), wide_halves(own)], axis=0)
    next_ref[...] = base_ref[...] - fold(dot(sel_ref[:, face:], both))


def far_kernel(coeff_ref, hi_ref, lo_ref, base_ref, next_ref):
    next_ref[...] = base_ref[...] - split_product(hi_ref[...], lo_ref[...], wide_halves(coeff_ref[...]))


def final_kernel(sum_ref, back_ref, sel_ref, base_ref, x_ref, scale_ref, up_ref, res_ref):
    face = back_ref.shape[0]
    both = jnp.concatenate([wide_halves(back_ref[...]), wide_halves(inside_part(sum_ref))], axis=0)
    res = base_ref[...] - fold(dot(sel_ref[:, : 2 * face], both))
    res_ref[...] = res
    up_ref[...] = x_ref[...] + scale_ref[...] * res


def call(kernel, name, outs, operands, in_specs=None, out_specs=None, scratch=(), spaces=None):
    return pl.pallas_call(
        kernel,
        out_shape=tuple(
            space(s, t) for space, (s, t) in zip(spaces or [pltpu.VMEM] * len(outs), outs)
        ),
        in_specs=in_specs or [VMEM] * len(operands),
        out_specs=tuple(out_specs or [VMEM] * len(outs)),
        scratch_shapes=list(scratch),
        compiler_params=pltpu.CompilerParams(vmem_limit_bytes=40 * 2**20),
        name=name,
    )(*operands)


def body(iterate, rhs, schur, near_block, u_basis, v_basis, tile_rank, send_rows, send_count, precond):
    n_rows, loads = iterate.shape
    face = send_rows.shape[2]
    tiles, top, _ = u_basis.shape
    size = lax.axis_size("wide")
    parts = lax.axis_size("groups")
    inside = [(i, i ^ 1) for i in range(size) if i ^ 1 < size]
    across = [(g * size + i, g * size + (i - 1 if i % 2 == 0 else i + 1)) for g in range(parts) for i in range(1, size - 1)]
    across += [(g * size + i, (g + 1) % parts * size + i) for g in range(parts) for i in (0, size - 1)]
    schur = schur.reshape(3 * face, 3 * face)
    block = ((face, loads), f32)
    field = ((n_rows, loads), f32)
    factor = ((n_rows, tiles * top), bf16)
    steps = tiles // tiles_at_once(tiles, top)

    arrays = (
        iterate,
        v_basis,
        send_rows.reshape(3, 1, face),
        send_count.reshape(3),
        tile_rank.reshape(tiles),
        schur,
        u_basis,
        near_block,
        rhs,
        precond.reshape(1, n_rows),
    )
    square = lambda a: (a.shape, a.dtype)
    coeff, out_a, out_m, out_b, corner, sel, x, schur, u, near, rhs, p = call(
        send_kernel,
        "send",
        [((tiles, top, loads), f32), block, block, block, ((face, face), f32), ((n_rows, 3 * face), bf16), field]
        + [square(arrays[i]) for i in (5, 6, 7, 8, 9)],
        [pltpu.with_memory_space_constraint(a, pltpu.HBM) for a in arrays],
        [HBM] * len(arrays),
        [HBM] + [VMEM] * 11,
        [
            pltpu.VMEM((tiles, top, n_rows), f32),
            pltpu.VMEM((3, 1, face), jnp.int32),
            pltpu.SMEM((3,), jnp.int32),
            pltpu.SMEM((tiles,), jnp.int32),
            pltpu.VMEM((tiles, top, loads), f32),
            pltpu.SemaphoreType.DMA((len(arrays),)),
            pltpu.SemaphoreType.DMA((steps,)),
        ],
        [pltpu.HBM] + [pltpu.VMEM] * 11,
    )
    gathered = lax.all_to_all(
        coeff, "wide", split_axis=0, concat_axis=0, tiled=True, axis_index_groups=[group_order(size)]
    )
    in_a = lax.ppermute(out_a, "wide", inside)
    got = lax.ppermute(out_b, ("groups", "wide"), across)
    corner = lax.ppermute(corner, ("groups", "wide"), across)
    pay, part = call(across_kernel, "across", [block, ((2 * face, loads), f32)], (in_a, out_m, schur))
    sums = lax.ppermute(pay, ("groups", "wide"), across)
    base, u_hi, u_lo, scale = call(
        base_kernel, "base", [field, factor, factor, field], (rhs, near, x, u, p, part)
    )
    (f_a,) = call(force_kernel, "force", [block], (got, part, schur, base))
    back = lax.ppermute(f_a, "wide", inside)
    (base,) = call(own_kernel, "own", [field], (got, corner, out_b, part, schur, sel, base))
    (base,) = call(far_kernel, "far", [field], (gathered.reshape(tiles * top, loads), u_hi, u_lo, base))
    return call(
        final_kernel,
        "final",
        [field, field],
        (sums, back, sel, base, x, scale),
        spaces=[jax.ShapeDtypeStruct] * 2,
    )


def solution(mesh):
    rows = P(("groups", "wide"), None)
    block = P(("groups", "wide"), None, None)
    basis = P("groups", None, "wide")
    in_specs = (rows, rows, block, rows, basis, basis, P("groups", "wide"), block, rows, P(("groups", "wide")))
    return jax.shard_map(body, mesh=mesh, in_specs=in_specs, out_specs=(rows, rows), check_vma=False)
```
